512 devices in a mesh: dp: 32 (over y, x, core), seq: 16 (over z).
Axes of the slice: x: 4, y: 4, z: 16, core: 2. Of those that a mesh axis runs over, the one named last changes fastest.
Arguments:
- big_qkv: bfloat16 [32768, 3840], P(('dp', 'seq')), may hold values from -6 to 6
- big_grad: bfloat16 [32768, 1280], P(('dp', 'seq')), may hold values from -18 to 18
- small_qkv: bfloat16 [65536, 3840], P(('dp', 'seq')), may hold values from -6 to 6
- small_grad: bfloat16 [65536, 1280], P(('dp', 'seq')), may hold values from -18 to 18
- small_ids: int32 [512, 128], P(('dp', 'seq')), may hold values from 0 to 1, as said below
Outputs:
- big_dqkv: bfloat16 [32768, 3840], P(('dp', 'seq'))
- small_dqkv: bfloat16 [65536, 3840], P(('dp', 'seq'))
- query_bias_grad: float32 [1280], replicated
The draws below stay inside these ranges and needn't reach their ends.
Inputs may be any that keep to these rules, and one draw needn't show every extreme that they name: `small_ids`: the rows of one device form one image of 128 patches (all 0), or two images of 64 patches each (0 then 1).
All inputs are finite; a program needn't handle non-finite values.
Results may differ from the reference program's by a relative error of at most 0.0067.
Values may be sent and summed in bfloat16 or wider, within the bound.
No kernel may reach another device: no remote copies, remote signals or barrier semaphores. Data moves between devices by JAX's collectives and lax.ppermute only.
A program may use at most 128 MiB of HBM per device.

```python
import jax
import jax.numpy as jnp
from jax import lax

HEADS = 16
HEAD = 80
D = 1280
BIG = 1024
SMALL_DEV = 128
N_DP = 32
DEVICES = 512


def drawn_features(key, total_rows):
    values = jax.random.normal(key, (total_rows, 3 * HEADS * HEAD), jnp.float32)
    return jnp.clip(values, -6.0, 6.0)


def rising(total_rows):
    return 1.0 + 2.0 * jnp.arange(total_rows, dtype=jnp.float32)[:, None] / total_rows


def normal_grads(key, total_rows):
    values = jnp.clip(jax.random.normal(key, (total_rows, HEADS * HEAD), jnp.float32), -6.0, 6.0)
    return values * rising(total_rows)


def draw_big_qkv(key, part):
    key = jax.random.fold_in(key, 11)
    total_rows = N_DP * BIG
    return drawn_features(key, total_rows).astype(jnp.bfloat16)


def draw_small_qkv(key, part):
    key = jax.random.fold_in(key, 13)
    total_rows = DEVICES * SMALL_DEV
    return drawn_features(key, total_rows).astype(jnp.bfloat16)


def draw_big_grad(key, part):
    key = jax.random.fold_in(key, 17)
    total_rows = N_DP * BIG
    return normal_grads(key, total_rows).astype(jnp.bfloat16)


def draw_small_grad(key, part):
    key = jax.random.fold_in(key, 19)
    total_rows = DEVICES * SMALL_DEV
    return normal_grads(key, total_rows).astype(jnp.bfloat16)


def draw_small_ids(key, part):
    key = jax.random.fold_in(key, 23)
    doubled = jax.random.randint(key, (DEVICES, 1), 0, 2)
    position = jnp.arange(SMALL_DEV)[None, :]
    return jnp.where((doubled == 1) & (position >= SMALL_DEV // 2), 1, 0).astype(jnp.int32)


def setup_inputs(seed: int = 0) -> dict:
    splits = jax.random.split(jax.random.key(seed), 6)
    big_qkv = draw_big_qkv(jax.random.fold_in(splits[5], 71), 0)
    big_grad = draw_big_grad(jax.random.fold_in(splits[5], 71), 0)
    small_qkv = draw_small_qkv(jax.random.fold_in(splits[5], 71), 0)
    small_grad = draw_small_grad(jax.random.fold_in(splits[5], 71), 0)
    small_ids = draw_small_ids(jax.random.fold_in(splits[5], 71), 0)
    return {"big_qkv": big_qkv, "big_grad": big_grad, "small_qkv": small_qkv, "small_grad": small_grad, "small_ids": small_ids}


def head_grads(packed, grad_rows, allowed):
    query_rows = packed[:, :HEAD]
    key_rows = packed[:, HEAD:2 * HEAD]
    value_rows = packed[:, 2 * HEAD:]
    scaling = HEAD ** -0.5
    scores = jnp.dot(query_rows, key_rows.T, preferred_element_type=jnp.float32) * scaling
    if allowed is not None:
        scores = jnp.where(allowed, scores, -1e30)
    row_top = jnp.max(scores, axis=1, keepdims=True)
    exponent = jnp.exp(scores - row_top)
    attention = exponent / jnp.sum(exponent, axis=1, keepdims=True)
    weights = attention.astype(jnp.bfloat16)
    attended = jnp.dot(weights, value_rows, preferred_element_type=jnp.float32)
    row_delta = jnp.sum(grad_rows.astype(jnp.float32) * attended, axis=1, keepdims=True)
    upstream = jnp.dot(grad_rows, value_rows.T, preferred_element_type=jnp.float32)
    slopes = (attention * (upstream - row_delta)).astype(jnp.bfloat16)
    query_grad = (jnp.dot(slopes, key_rows, preferred_element_type=jnp.float32) * scaling).astype(jnp.bfloat16)
    key_grad = (jnp.dot(slopes.T, query_rows, preferred_element_type=jnp.float32) * scaling).astype(jnp.bfloat16)
    value_grad = jnp.dot(weights.T, grad_rows, preferred_element_type=jnp.float32).astype(jnp.bfloat16)
    return jnp.concatenate([query_grad, key_grad, value_grad], axis=1)


def image_grads(packed, grad_rows, allowed):
    length = packed.shape[0]
    per_head = jnp.transpose(packed.reshape(length, HEADS, 3 * HEAD), (1, 0, 2))
    grad_head = jnp.transpose(grad_rows.reshape(length, HEADS, HEAD), (1, 0, 2))
    result = lax.map(lambda couple: head_grads(couple[0], couple[1], allowed), (per_head, grad_head))
    return jnp.transpose(result, (1, 0, 2)).reshape(length, 3 * HEADS * HEAD)


def query_total(gradients):
    total_rows = gradients.shape[0]
    picked = gradients.reshape(total_rows, HEADS, 3 * HEAD)[:, :, :HEAD].astype(jnp.float32)
    return jnp.sum(picked, axis=0).reshape(HEADS * HEAD)


def reference(big_qkv, big_grad, small_qkv, small_grad, small_ids):
    big_in = big_qkv.reshape(N_DP, BIG, 3 * D)
    big_cot = big_grad.reshape(N_DP, BIG, D)
    big_out = lax.map(lambda couple: image_grads(couple[0], couple[1], None), (big_in, big_cot))
    big_out = big_out.reshape(N_DP * BIG, 3 * D)
    small_in = small_qkv.reshape(DEVICES, SMALL_DEV, 3 * D)
    small_cot = small_grad.reshape(DEVICES, SMALL_DEV, D)
    small_out = lax.map(lambda triple: image_grads(triple[0], triple[1], triple[2][:, None] == triple[2][None, :]), (small_in, small_cot, small_ids))
    small_out = small_out.reshape(DEVICES * SMALL_DEV, 3 * D)
    bias_grad = query_total(big_out) + query_total(small_out)
    return big_out, small_out, bias_grad
```

```python
import functools

import jax
import jax.numpy as jnp
from jax import lax
from jax.experimental import pallas as pl
from jax.experimental.pallas import tpu as pltpu
from jax.sharding import PartitionSpec as P

HEAD = 80
HEADS = 16
SCALE = HEAD ** (-0.5)
LANES = 128
IN_ROWS = 2 * HEAD
OUT_ROWS = 3 * HEAD // 2
SUM_ROWS = 8
BLOCK = 256
F32 = jnp.float32
BF16 = jnp.bfloat16


def dot(left, right, left_dim, right_dim):
    return lax.dot_general(
        left, right, (((left_dim,), (right_dim,)), ((), ())), preferred_element_type=F32
    )


def params(mebibytes):
    return pltpu.CompilerParams(vmem_limit_bytes=mebibytes * 1024 * 1024)


def vmem(count):
    return [pl.BlockSpec(memory_space=pltpu.VMEM)] * count


def pack_kernel(qkv_ref, grad_ref, out_ref):
    qkv = qkv_ref[...].T
    grad = grad_ref[...].T
    for head in range(HEADS):
        first = 3 * HEAD * head
        left = qkv[first : first + 2 * HEAD]
        right = jnp.concatenate(
            [qkv[first + 2 * HEAD : first + 3 * HEAD], grad[HEAD * head : HEAD * (head + 1)]], axis=0
        )
        out_ref[head] = jnp.concatenate([left, right], axis=1)


def slopes_of(scores, upstream):
    exponent = jnp.exp(scores - jnp.max(scores, axis=0, keepdims=True))
    probs = exponent * (1.0 / jnp.sum(exponent, axis=0, keepdims=True))
    delta = jnp.sum(probs * upstream, axis=0, keepdims=True)
    return probs.astype(BF16), (probs * (upstream - delta)).astype(BF16)


def small_kernel(qkv_ref, grad_ref, ids_ref, out_ref, sum_ref, qkv_t, grad_t, out_t):
    qkv_t[...] = qkv_ref[...].T
    grad_t[...] = grad_ref[...].T
    rows = qkv_ref.shape[0]
    ids = jnp.broadcast_to(ids_ref[...].astype(F32), (rows, rows))
    allowed = ids == ids.T
    ones = jnp.ones((8, rows), BF16)
    sum_ref[...] = jnp.zeros_like(sum_ref)
    for head in range(HEADS):
        first = 3 * HEAD * head
        query = qkv_t[first : first + HEAD]
        key = qkv_t[first + HEAD : first + 2 * HEAD]
        value = qkv_t[first + 2 * HEAD : first + 3 * HEAD]
        grad = grad_t[HEAD * head : HEAD * (head + 1)]
        scores = jnp.where(allowed, dot(key, query, 0, 0) * SCALE, -1e30)
        weights, slopes = slopes_of(scores, dot(value, grad, 0, 0))
        query_grad = (dot(key, slopes, 1, 0) * SCALE).astype(BF16)
        out_t[first : first + HEAD] = query_grad
        out_t[first + HEAD : first + 2 * HEAD] = (dot(query, slopes, 1, 1) * SCALE).astype(BF16)
        out_t[first + 2 * HEAD : first + 3 * HEAD] = dot(grad, weights, 1, 1).astype(BF16)
        sum_ref[head : head + 1, :HEAD] = dot(ones, query_grad, 1, 1)[:1]
    out_ref[...] = out_t[...].T


def thirds(row):
    high = row.astype(BF16)
    rest = row - high.astype(F32)
    middle = rest.astype(BF16)
    low = (rest - middle.astype(F32)).astype(BF16)
    return [high.astype(F32), middle.astype(F32), low.astype(F32)]


def big_kernel(in_ref, sums_ref, out_ref, feat, key_sum, value_sum, query_t):
    pairs = in_ref.shape[0] // 2
    half = LANES // 2
    for pair in range(pairs):
        one, two = in_ref[2 * pair], in_ref[2 * pair + 1]
        columns = slice(LANES * pair, LANES * (pair + 1))
        feat[:IN_ROWS, columns] = jnp.concatenate([one[:, :half], two[:, :half]], axis=1)
        feat[IN_ROWS:, columns] = jnp.concatenate([one[:, half:], two[:, half:]], axis=1)
    key = feat[HEAD : 2 * HEAD]
    key_rows = key.T
    value_rows = feat[2 * HEAD : 3 * HEAD].T
    length = key.shape[1]
    for start in range(0, length, BLOCK):
        columns = slice(start, start + BLOCK)
        query = feat[:HEAD, columns]
        grad = feat[3 * HEAD :, columns]
        scores = dot(key_rows, query, 1, 0) * SCALE
        weights, slopes = slopes_of(scores, dot(value_rows, grad, 1, 0))
        query_t[:, columns] = (dot(key, slopes, 1, 0) * SCALE).astype(BF16)
        key_part = dot(slopes, query.T, 1, 0)
        value_part = dot(weights, grad.T, 1, 0)
        if start == 0:
            key_sum[...] = key_part
            value_sum[...] = value_part
        else:
            key_sum[...] += key_part
            value_sum[...] += value_part
    query_grad = query_t[...]
    big_row = dot(jnp.ones((8, length), BF16), query_grad, 1, 1)[:1]
    big_row = jnp.concatenate([big_row, jnp.zeros((1, LANES - HEAD), F32)], axis=1)
    extra = jnp.concatenate(
        thirds(big_row) + thirds(sums_ref[...]) + [jnp.zeros((2, LANES), F32)], axis=0
    )
    whole = jnp.concatenate(
        [query_grad.astype(F32), (key_sum[...] * SCALE).T, value_sum[...].T], axis=0
    )
    for pair in range(pairs):
        block = whole[:, LANES * pair : LANES * (pair + 1)]
        upper, lower = block[:OUT_ROWS], block[OUT_ROWS:]
        one = jnp.concatenate([upper[:, :half], lower[:, :half]], axis=1)
        two = jnp.concatenate([upper[:, half:], lower[:, half:]], axis=1)
        out_ref[2 * pair] = jnp.concatenate([one, extra], axis=0).astype(BF16)
        out_ref[2 * pair + 1] = jnp.concatenate([two, extra], axis=0).astype(BF16)


def unpack_kernel(in_ref, out_ref):
    half = LANES // 2
    parts = []
    for head in range(HEADS):
        block = in_ref[head].astype(F32)[:OUT_ROWS]
        parts.append(jnp.concatenate([block[:, :half], block[:, half:]], axis=0).astype(BF16))
    out_ref[...] = jnp.concatenate(parts, axis=0).T


def call(kernel, shapes, count, scratch=(), mebibytes=32, flops=0, name=None):
    outs = vmem(len(shapes))
    return pl.pallas_call(
        kernel,
        out_shape=shapes if len(shapes) > 1 else shapes[0],
        in_specs=vmem(count),
        out_specs=outs if len(shapes) > 1 else outs[0],
        scratch_shapes=scratch,
        compiler_params=params(mebibytes),
        cost_estimate=pl.CostEstimate(flops=flops, bytes_accessed=2**20, transcendentals=0),
        name=name,
    )


def local(big_qkv, big_grad, small_qkv, small_grad, small_ids):
    rows = big_qkv.shape[0]
    small_rows = small_qkv.shape[0]
    images = lax.axis_size("dp")
    parts = lax.axis_size("seq")
    length = rows * parts
    width = 3 * HEAD * HEADS
    image = lax.axis_index("dp")

    sent = call(
        pack_kernel, [jax.ShapeDtypeStruct((HEADS, IN_ROWS, LANES), BF16)], 2, name="pack"
    )(big_qkv, big_grad)
    got = lax.all_to_all(sent, "seq", 0, 0, tiled=True)

    small_out, small_sum = call(
        small_kernel,
        [
            jax.ShapeDtypeStruct((small_rows, width), BF16),
            jax.ShapeDtypeStruct((HEADS, LANES), F32),
        ],
        3,
        [
            pltpu.VMEM((width, small_rows), BF16),
            pltpu.VMEM((HEAD * HEADS, small_rows), BF16),
            pltpu.VMEM((width, small_rows), BF16),
        ],
        flops=10**10,
        name="small",
    )(small_qkv, small_grad, small_ids)
    share = HEADS * LANES // images
    of_all = jnp.sum(lax.all_gather(small_sum, "dp", axis=0), axis=0).reshape(images, share)
    mine = lax.dynamic_index_in_dim(of_all, image, 0, keepdims=True)
    mine = jnp.concatenate([mine, jnp.zeros((1, LANES - share), F32)], axis=1)

    back = call(
        big_kernel,
        [jax.ShapeDtypeStruct((parts, OUT_ROWS + SUM_ROWS, LANES), BF16)],
        2,
        [
            pltpu.VMEM((4 * HEAD, length), BF16),
            pltpu.VMEM((length, HEAD), F32),
            pltpu.VMEM((length, HEAD), F32),
            pltpu.VMEM((HEAD, length), BF16),
        ],
        mebibytes=48,
        flops=10**10,
        name="big",
    )(got, mine)
    home = lax.all_to_all(back, "seq", 0, 0, tiled=True)

    extra = home[:, OUT_ROWS : OUT_ROWS + 6].astype(F32)
    big_sum = extra[:, 0] + extra[:, 1] + extra[:, 2]
    share_sum = jnp.sum(extra[:, 3] + extra[:, 4] + extra[:, 5], axis=0)[:share]
    total = big_sum.reshape(images, share) + jnp.where(
        jnp.arange(images)[:, None] == image, share_sum[None], 0.0
    )
    total = total.reshape(1, 1, HEADS * LANES)
    everyone = lax.all_to_all(
        jnp.broadcast_to(total, (images, 1, HEADS * LANES)), "dp", 0, 0, tiled=True
    )
    bias_grad = jnp.sum(everyone, axis=0).reshape(HEADS, LANES)[:, :HEAD].reshape(HEADS * HEAD)

    big_out = call(
        unpack_kernel, [jax.ShapeDtypeStruct((rows, width), BF16)], 1, flops=10**9, name="unpack"
    )(home)
    return big_out, small_out, bias_grad


def solution(mesh):
    spec = P(("dp", "seq"), None)
    return jax.shard_map(
        local,
        mesh=mesh,
        in_specs=(spec,) * 5,
        out_specs=(spec, spec, P()),
        check_vma=False,
    )
```

```python
import jax
import jax.numpy as jnp
from jax import lax
from jax.experimental import pallas as pl
from jax.experimental.pallas import tpu as pltpu
from jax.sharding import PartitionSpec as P

HEAD = 80
HEADS = 16
SCALE = HEAD ** (-0.5)
LANES = 128
IN_ROWS = 2 * HEAD
OUT_ROWS = 3 * HEAD // 2
SUM_ROWS = 8
STEPS = 2
SHARE = HEADS * HEAD // 2**STEPS
BLOCK = 256
F32 = jnp.float32
BF16 = jnp.bfloat16


def dot(left, right, left_dim, right_dim):
    return lax.dot_general(
        left, right, (((left_dim,), (right_dim,)), ((), ())), preferred_element_type=F32
    )


def params(mebibytes):
    return pltpu.CompilerParams(vmem_limit_bytes=mebibytes * 1024 * 1024)


def pack(qkv_ref, grad_ref, out_ref):
    qkv = qkv_ref[...].T
    grad = grad_ref[...].T
    for head in range(HEADS):
        first = 3 * HEAD * head
        left = qkv[first : first + 2 * HEAD]
        right = jnp.concatenate(
            [qkv[first + 2 * HEAD : first + 3 * HEAD], grad[HEAD * head : HEAD * (head + 1)]], axis=0
        )
        out_ref[head] = jnp.concatenate([left, right], axis=1)


def slopes_of(scores, upstream):
    exponent = jnp.exp(scores - jnp.max(scores, axis=0, keepdims=True))
    probs = exponent * (1.0 / jnp.sum(exponent, axis=0, keepdims=True))
    delta = jnp.sum(probs * upstream, axis=0, keepdims=True)
    return probs.astype(BF16), (probs * (upstream - delta)).astype(BF16)


def small_images(qkv_hbm, grad_hbm, ids_ref, out_hbm, sum_ref, scratch):
    qkv, grads, qkv_t, grad_t, out_t, out, query_t, sems = scratch
    loads = [
        pltpu.make_async_copy(qkv_hbm, qkv, sems.at[0]),
        pltpu.make_async_copy(grad_hbm, grads, sems.at[1]),
    ]
    for load in loads:
        load.start()
    rows = qkv.shape[0]
    ids = jnp.broadcast_to(ids_ref[...].astype(F32), (rows, rows))
    allowed = ids == ids.T
    for load in loads:
        load.wait()
    qkv_t[...] = qkv[...].T
    grad_t[...] = grads[...].T
    for head in range(HEADS):
        first = 3 * HEAD * head
        query = qkv_t[first : first + HEAD]
        key = qkv_t[first + HEAD : first + 2 * HEAD]
        value = qkv_t[first + 2 * HEAD : first + 3 * HEAD]
        grad = grad_t[HEAD * head : HEAD * (head + 1)]
        scores = jnp.where(allowed, dot(key, query, 0, 0) * SCALE, -1e30)
        weights, slopes = slopes_of(scores, dot(value, grad, 0, 0))
        query_grad = (dot(key, slopes, 1, 0) * SCALE).astype(BF16)
        out_t[first : first + HEAD] = query_grad
        query_t[HEAD * head : HEAD * (head + 1)] = query_grad
        out_t[first + HEAD : first + 2 * HEAD] = (dot(query, slopes, 1, 1) * SCALE).astype(BF16)
        out_t[first + 2 * HEAD : first + 3 * HEAD] = dot(grad, weights, 1, 1).astype(BF16)
    out[...] = out_t[...].T
    store = pltpu.make_async_copy(out, out_hbm, sems.at[0])
    store.start()
    sum_ref[...] = dot(jnp.ones((8, rows), BF16), query_t[...], 1, 1)[:1]
    store.wait()


def first_kernel(
    core_ref, qkv_hbm, grad_hbm, small_qkv, small_grad, ids_ref, out_ref, small_out, sum_ref, qkv, grad, sems, *scratch
):
    loads = [
        pltpu.make_async_copy(qkv_hbm, qkv, sems.at[0]),
        pltpu.make_async_copy(grad_hbm, grad, sems.at[1]),
    ]
    for load in loads:
        load.start()
    for load in loads:
        load.wait()
    pack(qkv, grad, out_ref)
    sum_ref[...] = jnp.zeros_like(sum_ref)

    @pl.when(core_ref[0] == 1)
    def _():
        small_images(small_qkv, small_grad, ids_ref, small_out, sum_ref, scratch)


def second_kernel(core_ref, small_qkv, small_grad, ids_ref, before, small_out, sum_ref, *scratch):
    sum_ref[...] = jnp.zeros_like(sum_ref)

    @pl.when(core_ref[0] == 0)
    def _():
        small_images(small_qkv, small_grad, ids_ref, small_out, sum_ref, scratch)


def pieces(row):
    high = row.astype(BF16).astype(F32)
    return jnp.concatenate([high, (row - high).astype(BF16).astype(F32)], axis=0)


def big_kernel(in_ref, sums_ref, out_ref, feat, key_sum, value_sum, query_t):
    pairs = in_ref.shape[0] // 2
    half = LANES // 2
    for pair in range(pairs):
        one, two = in_ref[2 * pair], in_ref[2 * pair + 1]
        columns = slice(LANES * pair, LANES * (pair + 1))
        feat[:IN_ROWS, columns] = jnp.concatenate([one[:, :half], two[:, :half]], axis=1)
        feat[IN_ROWS:, columns] = jnp.concatenate([one[:, half:], two[:, half:]], axis=1)
    key = feat[HEAD : 2 * HEAD]
    key_rows = key.T
    value_rows = feat[2 * HEAD : 3 * HEAD].T
    length = key.shape[1]
    for start in range(0, length, BLOCK):
        columns = slice(start, start + BLOCK)
        query = feat[:HEAD, columns]
        grad = feat[3 * HEAD :, columns]
        scores = dot(key_rows, query, 1, 0) * SCALE
        weights, slopes = slopes_of(scores, dot(value_rows, grad, 1, 0))
        query_t[:, columns] = (dot(key, slopes, 1, 0) * SCALE).astype(BF16)
        key_part = dot(slopes, query.T, 1, 0)
        value_part = dot(weights, grad.T, 1, 0)
        if start == 0:
            key_sum[...] = key_part
            value_sum[...] = value_part
        else:
            key_sum[...] += key_part
            value_sum[...] += value_part
    query_grad = query_t[...]
    big_row = dot(jnp.ones((8, length), BF16), query_grad, 1, 1)[:1]
    big_row = jnp.concatenate([big_row, jnp.zeros((1, LANES - HEAD), F32)], axis=1)
    extra = pieces(jnp.concatenate([sums_ref[...], big_row], axis=0))
    whole = jnp.concatenate(
        [query_grad.astype(F32), (key_sum[...] * SCALE).T, value_sum[...].T], axis=0
    )
    for pair in range(pairs):
        block = whole[:, LANES * pair : LANES * (pair + 1)]
        upper, lower = block[:OUT_ROWS], block[OUT_ROWS:]
        one = jnp.concatenate([upper[:, :half], lower[:, :half]], axis=1)
        two = jnp.concatenate([upper[:, half:], lower[:, half:]], axis=1)
        out_ref[2 * pair] = jnp.concatenate([one, extra], axis=0).astype(BF16)
        out_ref[2 * pair + 1] = jnp.concatenate([two, extra], axis=0).astype(BF16)


def unpack_kernel(in_ref, out_ref):
    half = LANES // 2
    parts = []
    for head in range(HEADS):
        block = in_ref[head].astype(F32)[:OUT_ROWS]
        parts.append(jnp.concatenate([block[:, :half], block[:, half:]], axis=0).astype(BF16))
    out_ref[...] = jnp.concatenate(parts, axis=0).T


def call(kernel, shapes, in_specs, out_specs, operands, scratch=(), mebibytes=60, flops=0, name=None, aliases=None):
    return pl.pallas_call(
        kernel,
        out_shape=shapes,
        in_specs=in_specs,
        out_specs=out_specs,
        scratch_shapes=scratch,
        compiler_params=params(mebibytes),
        cost_estimate=pl.CostEstimate(flops=flops, bytes_accessed=2**20, transcendentals=0),
        input_output_aliases=aliases or {},
        name=name,
    )(*operands)


VMEM = pl.BlockSpec(memory_space=pltpu.VMEM)
SMEM = pl.BlockSpec(memory_space=pltpu.SMEM)
ANY = pl.BlockSpec(memory_space=pl.ANY)


def halved(sums, image, images, core):
    for step in range(STEPS):
        bit = 2 << step
        half = sums.shape[0] // 2
        upper = (image // bit) % 2
        kept = lax.dynamic_slice(sums, (upper * half,), (half,))
        given = lax.dynamic_slice(sums, ((1 - upper) * half,), (half,))
        pairs = [(at, at ^ bit) for at in range(images) if at % 2 == core]
        sums = kept + lax.ppermute(given, "dp", pairs)
    return sums


def local(big_qkv, big_grad, small_qkv, small_grad, small_ids):
    rows = big_qkv.shape[0]
    small_rows = small_qkv.shape[0]
    images = lax.axis_size("dp")
    parts = lax.axis_size("seq")
    length = rows * parts
    width = 3 * HEAD * HEADS
    image = lax.axis_index("dp")
    core = jnp.reshape(image % 2, (1,)).astype(jnp.int32)

    small_scratch = [
        pltpu.VMEM((small_rows, width), BF16),
        pltpu.VMEM((small_rows, HEAD * HEADS), BF16),
        pltpu.VMEM((width, small_rows), BF16),
        pltpu.VMEM((HEAD * HEADS, small_rows), BF16),
        pltpu.VMEM((width, small_rows), BF16),
        pltpu.VMEM((small_rows, width), BF16),
        pltpu.VMEM((HEAD * HEADS, small_rows), BF16),
        pltpu.SemaphoreType.DMA((2,)),
    ]
    small_shape = jax.ShapeDtypeStruct((small_rows, width), BF16)
    sum_shape = jax.ShapeDtypeStruct((1, HEADS * HEAD), F32)
    sent, small_out, small_sum = call(
        first_kernel,
        [jax.ShapeDtypeStruct((HEADS, IN_ROWS, LANES), BF16), small_shape, sum_shape],
        [SMEM, ANY, ANY, ANY, ANY, VMEM],
        [VMEM, ANY, VMEM],
        (core, big_qkv, big_grad, small_qkv, small_grad, small_ids),
        [
            pltpu.VMEM((rows, width), BF16),
            pltpu.VMEM((rows, HEAD * HEADS), BF16),
            pltpu.SemaphoreType.DMA((2,)),
            *small_scratch,
        ],
        name="pack",
    )
    late_sums = halved(small_sum.reshape(HEADS * HEAD), image, images, 1)
    sent, late_sums = lax.optimization_barrier((sent, late_sums))
    got = lax.all_to_all(sent, "seq", 0, 0, tiled=True)

    small_out, small_sum = call(
        second_kernel,
        [small_shape, sum_shape],
        [SMEM, ANY, ANY, VMEM, ANY],
        [ANY, VMEM],
        (core, small_qkv, small_grad, small_ids, small_out),
        small_scratch,
        flops=10**10,
        name="small",
        aliases={4: 0},
    )

    sums = late_sums + halved(small_sum.reshape(HEADS * HEAD), image, images, 0)
    sums = jnp.pad(sums, (0, 3 * LANES - SHARE)).reshape(3, LANES)

    back = call(
        big_kernel,
        jax.ShapeDtypeStruct((parts, OUT_ROWS + SUM_ROWS, LANES), BF16),
        [VMEM, VMEM],
        VMEM,
        (got, sums),
        mebibytes=40,
        scratch=[
            pltpu.VMEM((4 * HEAD, length), BF16),
            pltpu.VMEM((length, HEAD), F32),
            pltpu.VMEM((length, HEAD), F32),
            pltpu.VMEM((HEAD, length), BF16),
        ],
        flops=10**10,
        name="big",
    )
    home = lax.all_to_all(back, "seq", 0, 0, tiled=True)

    extra = home[:, OUT_ROWS:].astype(F32)
    extra = extra[:, :4] + extra[:, 4:]
    share = jnp.sum(extra[:, :3], axis=0).reshape(3 * LANES)[:SHARE]
    held = jnp.arange(2**STEPS) == (image // 2 % 2) * 2 + image // 4 % 2
    total = extra[:, 3, :HEAD].reshape(HEADS * HEAD) + jnp.where(held[:, None], share, 0.0).reshape(HEADS * HEAD)
    everyone = lax.all_to_all(
        jnp.broadcast_to(total, (images, 1, HEADS * HEAD)), "dp", 0, 0, tiled=True
    )
    bias_grad = jnp.sum(everyone, axis=(0, 1))

    big_out = call(
        unpack_kernel,
        jax.ShapeDtypeStruct((rows, width), BF16),
        [VMEM],
        VMEM,
        (home,),
        mebibytes=32,
        flops=10**9,
        name="unpack",
    )
    return big_out, small_out, bias_grad


def solution(mesh):
    spec = P(("dp", "seq"), None)
    return jax.shard_map(
        local,
        mesh=mesh,
        in_specs=(spec,) * 5,
        out_specs=(spec, spec, P()),
        check_vma=False,
    )
```

```python
import math

import jax
import jax.numpy as jnp
from jax import lax
from jax.experimental import pallas as pl
from jax.experimental.pallas import tpu as pltpu
from jax.sharding import PartitionSpec as P

HEAD = 80
HEADS = 16
SCALE = HEAD ** (-0.5)
LANES = 128
IN_ROWS = 2 * HEAD
OUT_ROWS = 3 * HEAD // 2
SUM_ROWS = 8
STEPS = (((2, 2), (4, 4)), ((20, 4), (18, 2)))
SHARE = HEADS * HEAD // 4
EXPONENT = SCALE * math.log2(math.e)
F32 = jnp.float32
BF16 = jnp.bfloat16


def dot(left, right, left_dim, right_dim):
    return lax.dot_general(
        left, right, (((left_dim,), (right_dim,)), ((), ())), preferred_element_type=F32
    )


def params(mebibytes):
    return pltpu.CompilerParams(vmem_limit_bytes=mebibytes * 1024 * 1024)


def slopes_of(scores, upstream):
    exponent = jnp.exp2((scores - jnp.max(scores, axis=0, keepdims=True)) * EXPONENT)
    inverse = 1.0 / jnp.sum(exponent, axis=0, keepdims=True)
    delta = jnp.sum(exponent * upstream, axis=0, keepdims=True) * inverse
    probs = exponent * inverse
    return probs.astype(BF16), (probs * (upstream - delta)).astype(BF16)


def small_loads(qkv_hbm, grad_hbm, ids_hbm, scratch):
    sems = scratch[-1]
    sources = (qkv_hbm, grad_hbm, ids_hbm)
    return [pltpu.make_async_copy(sources[at], scratch[at], sems.at[at]) for at in range(3)]


def small_images(loads, out_hbm, kept_hbm, given_hbm, core, scratch):
    qkv, grads, ids_ref, qkv_t, grad_t, out_t, out, query_t, kept, given, sems = scratch
    rows = qkv.shape[0]
    for load in loads:
        load.wait()
    ids = jnp.broadcast_to(ids_ref[...].astype(F32), (rows, rows))
    allowed = ids == ids.T
    qkv_t[...] = qkv[...].T
    grad_t[...] = grads[...].T

    def part(head, which):
        first = 3 * HEAD * head + HEAD * which
        return qkv_t[first : first + HEAD]

    def grad(head):
        return grad_t[HEAD * head : HEAD * (head + 1)]

    heads = range(HEADS)
    scores = [jnp.where(allowed, dot(part(head, 1), part(head, 0), 0, 0), -1e30) for head in heads]
    upstream = [dot(part(head, 2), grad(head), 0, 0) for head in heads]
    both = [slopes_of(*pair) for pair in zip(scores, upstream)]
    query_grad = [(dot(part(head, 1), both[head][1], 1, 0) * SCALE).astype(BF16) for head in heads]
    key_grad = [(dot(part(head, 0), both[head][1], 1, 1) * SCALE).astype(BF16) for head in heads]
    value_grad = [dot(grad(head), both[head][0], 1, 1).astype(BF16) for head in heads]
    for head in heads:
        first = 3 * HEAD * head
        out_t[first : first + HEAD] = query_grad[head]
        query_t[HEAD * head : HEAD * (head + 1)] = query_grad[head]
        out_t[first + HEAD : first + 2 * HEAD] = key_grad[head]
        out_t[first + 2 * HEAD : first + 3 * HEAD] = value_grad[head]
    sums = dot(jnp.ones((8, rows), BF16), query_t[...], 1, 1)[:1]
    half = HEADS * HEAD // 2
    upper = lax.axis_index("dp") // STEPS[core][0][1] % 2
    kept[...] = jnp.where(upper == 1, sums[:, half:], sums[:, :half])
    given[...] = jnp.where(upper == 1, sums[:, :half], sums[:, half:])
    out[...] = out_t[...].T
    stores = [
        pltpu.make_async_copy(out, out_hbm, sems.at[0]),
        pltpu.make_async_copy(kept, kept_hbm, sems.at[1]),
        pltpu.make_async_copy(given, given_hbm, sems.at[2]),
    ]
    for store in stores:
        store.start()
    for store in stores:
        store.wait()


def first_kernel(
    qkv_hbm,
    grad_hbm,
    small_qkv,
    small_grad,
    ids_hbm,
    out_hbm,
    small_out,
    kept_hbm,
    given_hbm,
    qkv,
    grad,
    packed,
    in_sems,
    out_sems,
    *scratch,
):
    parts = in_sems.shape[1]
    heads = HEADS // parts
    wide, narrow = 3 * HEAD * heads, HEAD * heads
    loads = []
    for part in range(parts):
        columns = pl.ds(part * wide, wide)
        loads.append(
            pltpu.make_async_copy(qkv_hbm.at[:, columns], qkv.at[:, columns], in_sems.at[0, part])
        )
        columns = pl.ds(part * narrow, narrow)
        loads.append(
            pltpu.make_async_copy(grad_hbm.at[:, columns], grad.at[:, columns], in_sems.at[1, part])
        )
    for load in loads:
        load.start()
    late = lax.axis_index("dp") % 2 == 1
    after = small_loads(small_qkv, small_grad, ids_hbm, scratch)

    @pl.when(late)
    def _():
        for load in after:
            load.start()

    stores = []
    for part in range(parts):
        loads[2 * part].wait()
        loads[2 * part + 1].wait()
        turned = qkv[:, part * wide : (part + 1) * wide].T
        turned_grad = grad[:, part * narrow : (part + 1) * narrow].T
        for index in range(heads):
            first = 3 * HEAD * index
            left = turned[first : first + 2 * HEAD]
            right = jnp.concatenate(
                [
                    turned[first + 2 * HEAD : first + 3 * HEAD],
                    turned_grad[HEAD * index : HEAD * (index + 1)],
                ],
                axis=0,
            )
            packed[part * heads + index] = jnp.concatenate([left, right], axis=1)
        done = pl.ds(part * heads, heads)
        stores.append(pltpu.make_async_copy(packed.at[done], out_hbm.at[done], out_sems.at[part]))
        stores[-1].start()

    @pl.when(late)
    def _():
        small_images(after, small_out, kept_hbm, given_hbm, 1, scratch)

    for store in stores:
        store.wait()


def second_kernel(
    small_qkv, small_grad, ids_hbm, before, small_out, kept_hbm, given_hbm, *scratch
):
    @pl.when(lax.axis_index("dp") % 2 == 0)
    def _():
        loads = small_loads(small_qkv, small_grad, ids_hbm, scratch)
        for load in loads:
            load.start()
        small_images(loads, small_out, kept_hbm, given_hbm, 0, scratch)


def pieces(row):
    high = row.astype(BF16).astype(F32)
    return jnp.concatenate([high, (row - high).astype(BF16).astype(F32)], axis=0)


def big_kernel(in_ref, sums_ref, out_ref, feat):
    pairs = in_ref.shape[0] // 2
    half = LANES // 2
    for pair in range(pairs):
        one, two = in_ref[2 * pair], in_ref[2 * pair + 1]
        columns = slice(LANES * pair, LANES * (pair + 1))
        feat[:IN_ROWS, columns] = jnp.concatenate([one[:, :half], two[:, :half]], axis=1)
        feat[IN_ROWS:, columns] = jnp.concatenate([one[:, half:], two[:, half:]], axis=1)
    query, key, value, grad = (feat[HEAD * which : HEAD * (which + 1)] for which in range(4))
    length = key.shape[1]
    weights, slopes = slopes_of(dot(key.T, query, 1, 0), dot(value.T, grad, 1, 0))
    query_grad = (dot(key, slopes, 1, 0) * SCALE).astype(BF16)
    key_grad = dot(query, slopes, 1, 1) * SCALE
    value_grad = dot(grad, weights, 1, 1)
    big_row = dot(jnp.ones((8, length), BF16), query_grad, 1, 1)[:1]
    big_row = jnp.concatenate([big_row, jnp.zeros((1, LANES - HEAD), F32)], axis=1)
    extra = pieces(jnp.concatenate([sums_ref[...], big_row], axis=0))
    whole = jnp.concatenate([query_grad.astype(F32), key_grad, value_grad], axis=0)
    for pair in range(pairs):
        block = whole[:, LANES * pair : LANES * (pair + 1)]
        upper, lower = block[:OUT_ROWS], block[OUT_ROWS:]
        one = jnp.concatenate([upper[:, :half], lower[:, :half]], axis=1)
        two = jnp.concatenate([upper[:, half:], lower[:, half:]], axis=1)
        out_ref[2 * pair] = jnp.concatenate([one, extra], axis=0).astype(BF16)
        out_ref[2 * pair + 1] = jnp.concatenate([two, extra], axis=0).astype(BF16)


def unpack_kernel(in_ref, out_ref):
    half = LANES // 2
    parts = []
    for head in range(HEADS):
        block = in_ref[head].astype(F32)[:OUT_ROWS]
        parts.append(jnp.concatenate([block[:, :half], block[:, half:]], axis=0).astype(BF16))
    out_ref[...] = jnp.concatenate(parts, axis=0).T


def call(kernel, shapes, in_specs, out_specs, operands, scratch=(), mebibytes=60, flops=0, name=None, aliases=None):
    return pl.pallas_call(
        kernel,
        out_shape=shapes,
        in_specs=in_specs,
        out_specs=out_specs,
        scratch_shapes=scratch,
        compiler_params=params(mebibytes),
        cost_estimate=pl.CostEstimate(flops=flops, bytes_accessed=2**20, transcendentals=0),
        input_output_aliases=aliases or {},
        name=name,
    )(*operands)


VMEM = pl.BlockSpec(memory_space=pltpu.VMEM)
ANY = pl.BlockSpec(memory_space=pl.ANY)


def summed(kept, given, image, images, core):
    (first, _), (second, bit) = STEPS[core]
    pairs = [[(at, at ^ step) for at in range(images) if at % 2 == core] for step in (first, second)]
    sums = (kept + lax.ppermute(given, "dp", pairs[0])).reshape(2 * SHARE)
    upper = image // bit % 2
    kept = lax.dynamic_slice(sums, (upper * SHARE,), (SHARE,))
    given = lax.dynamic_slice(sums, ((1 - upper) * SHARE,), (SHARE,))
    sums = kept + lax.ppermute(given, "dp", pairs[1])
    return jnp.where(image % 2 == core, sums, 0.0)


def local(big_qkv, big_grad, small_qkv, small_grad, small_ids):
    rows = big_qkv.shape[0]
    small_rows = small_qkv.shape[0]
    images = lax.axis_size("dp")
    parts = lax.axis_size("seq")
    length = rows * parts
    width = 3 * HEAD * HEADS
    image = lax.axis_index("dp")

    small_scratch = [
        pltpu.VMEM((small_rows, width), BF16),
        pltpu.VMEM((small_rows, HEAD * HEADS), BF16),
        pltpu.VMEM((1, small_rows), jnp.int32),
        pltpu.VMEM((width, small_rows), BF16),
        pltpu.VMEM((HEAD * HEADS, small_rows), BF16),
        pltpu.VMEM((width, small_rows), BF16),
        pltpu.VMEM((small_rows, width), BF16),
        pltpu.VMEM((HEAD * HEADS, small_rows), BF16),
        pltpu.VMEM((1, HEAD * HEADS // 2), F32),
        pltpu.VMEM((1, HEAD * HEADS // 2), F32),
        pltpu.SemaphoreType.DMA((3,)),
    ]
    small_shape = jax.ShapeDtypeStruct((small_rows, width), BF16)
    sum_shapes = [jax.ShapeDtypeStruct((1, HEADS * HEAD // 2), F32)] * 2
    sent, small_out, *sums = call(
        first_kernel,
        [jax.ShapeDtypeStruct((HEADS, IN_ROWS, LANES), BF16), small_shape, *sum_shapes],
        [ANY] * 5,
        [ANY] * 4,
        (big_qkv, big_grad, small_qkv, small_grad, small_ids),
        [
            pltpu.VMEM((rows, width), BF16),
            pltpu.VMEM((rows, HEAD * HEADS), BF16),
            pltpu.VMEM((HEADS, IN_ROWS, LANES), BF16),
            pltpu.SemaphoreType.DMA((2, 2)),
            pltpu.SemaphoreType.DMA((2,)),
            *small_scratch,
        ],
        name="pack",
    )
    late_sums = summed(*sums, image, images, 1)
    sent, late_sums = lax.optimization_barrier((sent, late_sums))
    got = lax.all_to_all(sent, "seq", 0, 0, tiled=True)

    small_out, *sums = call(
        second_kernel,
        [small_shape, *sum_shapes],
        [ANY] * 4,
        [ANY] * 3,
        (small_qkv, small_grad, small_ids, small_out),
        small_scratch,
        flops=10**10,
        name="small",
        aliases={3: 0},
    )

    sums = late_sums + summed(*sums, image, images, 0)
    sums = jnp.pad(sums, (0, 3 * LANES - SHARE)).reshape(3, LANES)

    back = call(
        big_kernel,
        jax.ShapeDtypeStruct((parts, OUT_ROWS + SUM_ROWS, LANES), BF16),
        [VMEM, VMEM],
        VMEM,
        (got, sums),
        mebibytes=40,
        scratch=[pltpu.VMEM((4 * HEAD, length), BF16)],
        flops=10**10,
        name="big",
    )
    home = lax.all_to_all(back, "seq", 0, 0, tiled=True)

    extra = home[:, OUT_ROWS:].astype(F32)
    extra = extra[:, :4] + extra[:, 4:]
    share = jnp.sum(extra[:, :3], axis=0).reshape(3 * LANES)[:SHARE]
    quarters = [image // first % 2 * 2 + image // second % 2 for (_, first), (_, second) in STEPS]
    held = jnp.arange(4) == jnp.where(image % 2 == 0, *quarters)
    total = extra[:, 3, :HEAD].reshape(HEADS * HEAD) + jnp.where(held[:, None], share, 0.0).reshape(HEADS * HEAD)
    everyone = lax.all_to_all(
        jnp.broadcast_to(total, (images, 1, HEADS * HEAD)), "dp", 0, 0, tiled=True
    )
    bias_grad = jnp.sum(everyone, axis=(0, 1))

    big_out = call(
        unpack_kernel,
        jax.ShapeDtypeStruct((rows, width), BF16),
        [VMEM],
        VMEM,
        (home,),
        mebibytes=32,
        flops=10**9,
        name="unpack",
    )
    return big_out, small_out, bias_grad


def solution(mesh):
    spec = P(("dp", "seq"), None)
    return jax.shard_map(
        local,
        mesh=mesh,
        in_specs=(spec,) * 5,
        out_specs=(spec, spec, P()),
        check_vma=False,
    )
```

```python
import math

import jax
import jax.numpy as jnp
from jax import lax
from jax.experimental import pallas as pl
from jax.experimental.pallas import tpu as pltpu
from jax.sharding import PartitionSpec as P

HEAD = 80
HEADS = 16
SCALE = HEAD ** (-0.5)
LANES = 128
TOGETHER = 1
IN_ROWS = 2 * HEAD
OUT_ROWS = 3 * HEAD // 2
SUM_ROWS = 8
STEPS = (((2, 2), (4, 4)), ((20, 4), (2, 2)))
SHARE = HEADS * HEAD // 4
EXPONENT = SCALE * math.log2(math.e)
F32 = jnp.float32
BF16 = jnp.bfloat16


def dot(left, right, left_dim, right_dim):
    return lax.dot_general(
        left, right, (((left_dim,), (right_dim,)), ((), ())), preferred_element_type=F32
    )


def params(mebibytes):
    return pltpu.CompilerParams(vmem_limit_bytes=mebibytes * 1024 * 1024)


def slopes_of(scores, upstream):
    exponent = jnp.exp2((scores - jnp.max(scores, axis=0, keepdims=True)) * EXPONENT)
    inverse = 1.0 / jnp.sum(exponent, axis=0, keepdims=True)
    delta = jnp.sum(exponent * upstream, axis=0, keepdims=True) * inverse
    probs = exponent * inverse
    return probs.astype(BF16), (probs * (upstream - delta)).astype(BF16)


def small_loads(qkv_hbm, grad_hbm, ids_hbm, scratch):
    sems = scratch[-1]
    sources = (qkv_hbm, grad_hbm, ids_hbm)
    return [pltpu.make_async_copy(sources[at], scratch[at], sems.at[at]) for at in range(3)]


def small_images(loads, out_hbm, kept_hbm, given_hbm, core, together, scratch):
    qkv, grads, ids_ref, qkv_t, grad_t, out_t, out, query_t, kept, given, sems = scratch
    rows = qkv.shape[0]
    for load in loads:
        load.wait()
    ids = jnp.broadcast_to(ids_ref[...].astype(F32), (rows, rows))
    allowed = ids == ids.T
    qkv_t[...] = qkv[...].T
    grad_t[...] = grads[...].T

    def place(head, which=0, count=3):
        first = count * HEAD * head + HEAD * which
        return pl.ds(first if isinstance(first, int) else pl.multiple_of(first, 16), HEAD)

    def some(heads):
        query, key, value = ([qkv_t[place(head, which)] for head in heads] for which in range(3))
        grad = [grad_t[place(head, 0, 1)] for head in heads]
        scores = [jnp.where(allowed, dot(*pair, 0, 0), -1e30) for pair in zip(key, query)]
        upstream = [dot(*pair, 0, 0) for pair in zip(value, grad)]
        weights, slopes = zip(*[slopes_of(*pair) for pair in zip(scores, upstream)])
        query_grad = [(dot(*pair, 1, 0) * SCALE).astype(BF16) for pair in zip(key, slopes)]
        key_grad = [(dot(*pair, 1, 1) * SCALE).astype(BF16) for pair in zip(query, slopes)]
        value_grad = [dot(*pair, 1, 1).astype(BF16) for pair in zip(grad, weights)]
        for at, head in enumerate(heads):
            query_t[place(head, 0, 1)] = query_grad[at]
            for which, result in enumerate((query_grad, key_grad, value_grad)):
                out_t[place(head, which)] = result[at]

    if together == HEADS:
        some(range(HEADS))
    else:

        @pl.loop(0, HEADS // together)
        def _(step):
            some([step * together + at for at in range(together)])

    sums = dot(jnp.ones((8, rows), BF16), query_t[...], 1, 1)[:1]
    half = HEADS * HEAD // 2
    upper = lax.axis_index("dp") // STEPS[core][0][1] % 2
    kept[...] = jnp.where(upper == 1, sums[:, half:], sums[:, :half])
    given[...] = jnp.where(upper == 1, sums[:, :half], sums[:, half:])
    out[...] = out_t[...].T
    stores = [
        pltpu.make_async_copy(out, out_hbm, sems.at[0]),
        pltpu.make_async_copy(kept, kept_hbm, sems.at[1]),
        pltpu.make_async_copy(given, given_hbm, sems.at[2]),
    ]
    for store in stores:
        store.start()
    for store in stores:
        store.wait()


def first_kernel(
    qkv_hbm,
    grad_hbm,
    small_qkv,
    small_grad,
    ids_hbm,
    out_hbm,
    small_out,
    kept_hbm,
    given_hbm,
    qkv,
    grad,
    packed,
    in_sems,
    out_sems,
    *scratch,
):
    parts = in_sems.shape[1]
    heads = HEADS // parts
    wide, narrow = 3 * HEAD * heads, HEAD * heads
    loads = []
    for part in range(parts):
        columns = pl.ds(part * wide, wide)
        loads.append(
            pltpu.make_async_copy(qkv_hbm.at[:, columns], qkv.at[:, columns], in_sems.at[0, part])
        )
        columns = pl.ds(part * narrow, narrow)
        loads.append(
            pltpu.make_async_copy(grad_hbm.at[:, columns], grad.at[:, columns], in_sems.at[1, part])
        )
    for load in loads:
        load.start()
    late = lax.axis_index("dp") % 2 == 1
    after = small_loads(small_qkv, small_grad, ids_hbm, scratch)

    @pl.when(late)
    def _():
        for load in after:
            load.start()

    stores = []
    for part in range(parts):
        loads[2 * part].wait()
        loads[2 * part + 1].wait()
        turned = qkv[:, part * wide : (part + 1) * wide].T
        turned_grad = grad[:, part * narrow : (part + 1) * narrow].T
        for index in range(heads):
            first = 3 * HEAD * index
            left = turned[first : first + 2 * HEAD]
            right = jnp.concatenate(
                [
                    turned[first + 2 * HEAD : first + 3 * HEAD],
                    turned_grad[HEAD * index : HEAD * (index + 1)],
                ],
                axis=0,
            )
            packed[part * heads + index] = jnp.concatenate([left, right], axis=1)
        done = pl.ds(part * heads, heads)
        stores.append(pltpu.make_async_copy(packed.at[done], out_hbm.at[done], out_sems.at[part]))
        stores[-1].start()

    @pl.when(late)
    def _():
        small_images(after, small_out, kept_hbm, given_hbm, 1, TOGETHER, scratch)

    for store in stores:
        store.wait()


def second_kernel(
    small_qkv, small_grad, ids_hbm, before, kept_before, given_before, small_out, kept_hbm, given_hbm, *scratch
):
    @pl.when(lax.axis_index("dp") % 2 == 0)
    def _():
        loads = small_loads(small_qkv, small_grad, ids_hbm, scratch)
        for load in loads:
            load.start()
        small_images(loads, small_out, kept_hbm, given_hbm, 0, HEADS, scratch)


def pieces(row):
    high = row.astype(BF16).astype(F32)
    return jnp.concatenate([high, (row - high).astype(BF16).astype(F32)], axis=0)


def big_kernel(in_ref, sums_ref, out_ref, feat):
    pairs = in_ref.shape[0] // 2
    half = LANES // 2
    for pair in range(pairs):
        one, two = in_ref[2 * pair], in_ref[2 * pair + 1]
        columns = slice(LANES * pair, LANES * (pair + 1))
        feat[:IN_ROWS, columns] = jnp.concatenate([one[:, :half], two[:, :half]], axis=1)
        feat[IN_ROWS:, columns] = jnp.concatenate([one[:, half:], two[:, half:]], axis=1)
    query, key, value, grad = (feat[HEAD * which : HEAD * (which + 1)] for which in range(4))
    length = key.shape[1]
    weights, slopes = slopes_of(dot(key.T, query, 1, 0), dot(value.T, grad, 1, 0))
    query_grad = (dot(key, slopes, 1, 0) * SCALE).astype(BF16)
    key_grad = dot(query, slopes, 1, 1) * SCALE
    value_grad = dot(grad, weights, 1, 1)
    big_row = dot(jnp.ones((8, length), BF16), query_grad, 1, 1)[:1]
    big_row = jnp.concatenate([big_row, jnp.zeros((1, LANES - HEAD), F32)], axis=1)
    extra = pieces(jnp.concatenate([sums_ref[...], big_row], axis=0))
    whole = jnp.concatenate([query_grad.astype(F32), key_grad, value_grad], axis=0)
    for pair in range(pairs):
        block = whole[:, LANES * pair : LANES * (pair + 1)]
        upper, lower = block[:OUT_ROWS], block[OUT_ROWS:]
        one = jnp.concatenate([upper[:, :half], lower[:, :half]], axis=1)
        two = jnp.concatenate([upper[:, half:], lower[:, half:]], axis=1)
        out_ref[2 * pair] = jnp.concatenate([one, extra], axis=0).astype(BF16)
        out_ref[2 * pair + 1] = jnp.concatenate([two, extra], axis=0).astype(BF16)


def unpack_kernel(in_ref, out_ref):
    half = LANES // 2
    parts = []
    for head in range(HEADS):
        block = in_ref[head].astype(F32)[:OUT_ROWS]
        parts.append(jnp.concatenate([block[:, :half], block[:, half:]], axis=0).astype(BF16))
    out_ref[...] = jnp.concatenate(parts, axis=0).T


def call(kernel, shapes, in_specs, out_specs, operands, scratch=(), mebibytes=60, flops=0, name=None, aliases=None):
    return pl.pallas_call(
        kernel,
        out_shape=shapes,
        in_specs=in_specs,
        out_specs=out_specs,
        scratch_shapes=scratch,
        compiler_params=params(mebibytes),
        cost_estimate=pl.CostEstimate(flops=flops, bytes_accessed=2**20, transcendentals=0),
        input_output_aliases=aliases or {},
        name=name,
    )(*operands)


VMEM = pl.BlockSpec(memory_space=pltpu.VMEM)
ANY = pl.BlockSpec(memory_space=pl.ANY)


def halved(given, images, step, cores):
    pairs = [(at, at ^ STEPS[at % 2][step][0]) for at in range(images) if at % 2 in cores]
    return lax.ppermute(given, "dp", pairs)


def local(big_qkv, big_grad, small_qkv, small_grad, small_ids):
    rows = big_qkv.shape[0]
    small_rows = small_qkv.shape[0]
    images = lax.axis_size("dp")
    parts = lax.axis_size("seq")
    length = rows * parts
    width = 3 * HEAD * HEADS
    image = lax.axis_index("dp")

    small_scratch = [
        pltpu.VMEM((small_rows, width), BF16),
        pltpu.VMEM((small_rows, HEAD * HEADS), BF16),
        pltpu.VMEM((1, small_rows), jnp.int32),
        pltpu.VMEM((width, small_rows), BF16),
        pltpu.VMEM((HEAD * HEADS, small_rows), BF16),
        pltpu.VMEM((width, small_rows), BF16),
        pltpu.VMEM((small_rows, width), BF16),
        pltpu.VMEM((HEAD * HEADS, small_rows), BF16),
        pltpu.VMEM((1, HEAD * HEADS // 2), F32),
        pltpu.VMEM((1, HEAD * HEADS // 2), F32),
        pltpu.SemaphoreType.DMA((3,)),
    ]
    small_shape = jax.ShapeDtypeStruct((small_rows, width), BF16)
    sum_shapes = [jax.ShapeDtypeStruct((1, HEADS * HEAD // 2), F32)] * 2
    sent, small_out, *sums = call(
        first_kernel,
        [jax.ShapeDtypeStruct((HEADS, IN_ROWS, LANES), BF16), small_shape, *sum_shapes],
        [ANY] * 5,
        [ANY] * 4,
        (big_qkv, big_grad, small_qkv, small_grad, small_ids),
        [
            pltpu.VMEM((rows, width), BF16),
            pltpu.VMEM((rows, HEAD * HEADS), BF16),
            pltpu.VMEM((HEADS, IN_ROWS, LANES), BF16),
            pltpu.SemaphoreType.DMA((2, 2)),
            pltpu.SemaphoreType.DMA((2,)),
            *small_scratch,
        ],
        name="pack",
    )
    late = halved(sums[1], images, 0, (1,))
    sent, late = lax.optimization_barrier((sent, late))
    got = lax.all_to_all(sent, "seq", 0, 0, tiled=True)

    small_out, *sums = call(
        second_kernel,
        [small_shape, *sum_shapes],
        [ANY] * 6,
        [ANY] * 3,
        (small_qkv, small_grad, small_ids, small_out, *sums),
        small_scratch,
        flops=10**10,
        name="small",
        aliases={3: 0, 4: 1, 5: 2},
    )

    early = halved(sums[1], images, 0, (0,))
    sums = (sums[0] + late + early).reshape(2 * SHARE)
    upper = jnp.where(image % 2 == 0, *[image // STEPS[core][1][1] % 2 for core in range(2)])
    kept = lax.dynamic_slice(sums, (upper * SHARE,), (SHARE,))
    given = lax.dynamic_slice(sums, ((1 - upper) * SHARE,), (SHARE,))
    sums = kept + halved(given, images, 1, (0, 1))
    sums = jnp.pad(sums, (0, 3 * LANES - SHARE)).reshape(3, LANES)

    back = call(
        big_kernel,
        jax.ShapeDtypeStruct((parts, OUT_ROWS + SUM_ROWS, LANES), BF16),
        [VMEM, VMEM],
        VMEM,
        (got, sums),
        mebibytes=40,
        scratch=[pltpu.VMEM((4 * HEAD, length), BF16)],
        flops=10**10,
        name="big",
    )
    home = lax.all_to_all(back, "seq", 0, 0, tiled=True)

    extra = home[:, OUT_ROWS:].astype(F32)
    extra = extra[:, :4] + extra[:, 4:]
    share = jnp.sum(extra[:, :3], axis=0).reshape(3 * LANES)[:SHARE]
    quarters = [image // first % 2 * 2 + image // second % 2 for (_, first), (_, second) in STEPS]
    held = jnp.arange(4) == jnp.where(image % 2 == 0, *quarters)
    total = extra[:, 3, :HEAD].reshape(HEADS * HEAD) + jnp.where(held[:, None], share, 0.0).reshape(HEADS * HEAD)
    everyone = lax.all_to_all(
        jnp.broadcast_to(total, (images, 1, HEADS * HEAD)), "dp", 0, 0, tiled=True
    )
    bias_grad = jnp.sum(everyone, axis=(0, 1))

    big_out = call(
        unpack_kernel,
        jax.ShapeDtypeStruct((rows, width), BF16),
        [VMEM],
        VMEM,
        (home,),
        mebibytes=32,
        flops=10**9,
        name="unpack",
    )
    return big_out, small_out, bias_grad


def solution(mesh):
    spec = P(("dp", "seq"), None)
    return jax.shard_map(
        local,
        mesh=mesh,
        in_specs=(spec,) * 5,
        out_specs=(spec, spec, P()),
        check_vma=False,
    )
```

```python
import math

import jax
import jax.numpy as jnp
from jax import lax
from jax.experimental import pallas as pl
from jax.experimental.pallas import tpu as pltpu
from jax.sharding import PartitionSpec as P

HEAD = 80
HEADS = 16
SCALE = HEAD ** (-0.5)
LANES = 128
FIRST_PART = 10
FIRST_IMAGE = 21
TOGETHER = 1
IN_ROWS = 2 * HEAD
OUT_ROWS = 3 * HEAD // 2
SUM_ROWS = 8
STEPS = (((2, 2), (4, 4)), ((20, 4), (2, 2)))
SHARE = HEADS * HEAD // 4
EXPONENT = SCALE * math.log2(math.e)
F32 = jnp.float32
BF16 = jnp.bfloat16


def dot(left, right, left_dim, right_dim):
    return lax.dot_general(
        left, right, (((left_dim,), (right_dim,)), ((), ())), preferred_element_type=F32
    )


def params(mebibytes):
    return pltpu.CompilerParams(vmem_limit_bytes=mebibytes * 1024 * 1024)


def slopes_of(scores, upstream):
    exponent = jnp.exp2((scores - jnp.max(scores, axis=0, keepdims=True)) * EXPONENT)
    inverse = 1.0 / jnp.sum(exponent, axis=0, keepdims=True)
    delta = jnp.sum(exponent * upstream, axis=0, keepdims=True) * inverse
    probs = exponent * inverse
    return probs.astype(BF16), (probs * (upstream - delta)).astype(BF16)


def small_loads(qkv_hbm, grad_hbm, ids_hbm, scratch):
    sems = scratch[-1]
    sources = (qkv_hbm, grad_hbm, ids_hbm)
    return [pltpu.make_async_copy(sources[at], scratch[at], sems.at[at]) for at in range(3)]


def small_images(loads, out_hbm, kept_hbm, given_hbm, core, together, scratch):
    qkv, grads, ids_ref, qkv_t, grad_t, out_t, out, query_t, kept, given, sems = scratch
    rows = qkv.shape[0]
    for load in loads:
        load.wait()
    ids = jnp.broadcast_to(ids_ref[...].astype(F32), (rows, rows))
    allowed = ids == ids.T
    qkv_t[...] = qkv[...].T
    grad_t[...] = grads[...].T

    def place(head, which=0, count=3):
        first = count * HEAD * head + HEAD * which
        return pl.ds(first if isinstance(first, int) else pl.multiple_of(first, 16), HEAD)

    def some(heads):
        query, key, value = ([qkv_t[place(head, which)] for head in heads] for which in range(3))
        grad = [grad_t[place(head, 0, 1)] for head in heads]
        scores = [jnp.where(allowed, dot(*pair, 0, 0), -1e30) for pair in zip(key, query)]
        upstream = [dot(*pair, 0, 0) for pair in zip(value, grad)]
        weights, slopes = zip(*[slopes_of(*pair) for pair in zip(scores, upstream)])
        query_grad = [(dot(*pair, 1, 0) * SCALE).astype(BF16) for pair in zip(key, slopes)]
        key_grad = [(dot(*pair, 1, 1) * SCALE).astype(BF16) for pair in zip(query, slopes)]
        value_grad = [dot(*pair, 1, 1).astype(BF16) for pair in zip(grad, weights)]
        for at, head in enumerate(heads):
            query_t[place(head, 0, 1)] = query_grad[at]
            for which, result in enumerate((query_grad, key_grad, value_grad)):
                out_t[place(head, which)] = result[at]

    if together == HEADS:
        some(range(HEADS))
    else:

        @pl.loop(0, HEADS // together)
        def _(step):
            some([step * together + at for at in range(together)])

    sums = dot(jnp.ones((8, rows), BF16), query_t[...], 1, 1)[:1]
    half = HEADS * HEAD // 2
    upper = lax.axis_index("dp") // STEPS[core][0][1] % 2
    kept[...] = jnp.where(upper == 1, sums[:, half:], sums[:, :half])
    given[...] = jnp.where(upper == 1, sums[:, :half], sums[:, half:])
    out[...] = out_t[...].T
    stores = [
        pltpu.make_async_copy(out, out_hbm, sems.at[0]),
        pltpu.make_async_copy(kept, kept_hbm, sems.at[1]),
        pltpu.make_async_copy(given, given_hbm, sems.at[2]),
    ]
    for store in stores:
        store.start()
    for store in stores:
        store.wait()


def first_kernel(
    qkv_hbm,
    grad_hbm,
    small_qkv,
    small_grad,
    ids_hbm,
    out_hbm,
    small_out,
    kept_hbm,
    given_hbm,
    qkv,
    grad,
    packed,
    in_sems,
    out_sems,
    *scratch,
):
    parts = in_sems.shape[1]
    heads = HEADS // parts
    wide, narrow = 3 * HEAD * heads, HEAD * heads
    loads = []
    for part in range(parts):
        columns = pl.ds(part * wide, wide)
        loads.append(
            pltpu.make_async_copy(qkv_hbm.at[:, columns], qkv.at[:, columns], in_sems.at[0, part])
        )
        columns = pl.ds(part * narrow, narrow)
        loads.append(
            pltpu.make_async_copy(grad_hbm.at[:, columns], grad.at[:, columns], in_sems.at[1, part])
        )
    for load in loads:
        load.start()
    late = lax.axis_index("dp") % 2 == 1
    after = small_loads(small_qkv, small_grad, ids_hbm, scratch)

    @pl.when(late)
    def _():
        for load in after:
            load.start()

    stores = []
    for part in range(parts):
        loads[2 * part].wait()
        loads[2 * part + 1].wait()
        turned = qkv[:, part * wide : (part + 1) * wide].T
        turned_grad = grad[:, part * narrow : (part + 1) * narrow].T
        for index in range(heads):
            first = 3 * HEAD * index
            left = turned[first : first + 2 * HEAD]
            right = jnp.concatenate(
                [
                    turned[first + 2 * HEAD : first + 3 * HEAD],
                    turned_grad[HEAD * index : HEAD * (index + 1)],
                ],
                axis=0,
            )
            packed[part * heads + index] = jnp.concatenate([left, right], axis=1)
        done = pl.ds(part * heads, heads)
        stores.append(pltpu.make_async_copy(packed.at[done], out_hbm.at[done], out_sems.at[part]))
        stores[-1].start()

    @pl.when(late)
    def _():
        small_images(after, small_out, kept_hbm, given_hbm, 1, TOGETHER, scratch)

    for store in stores:
        store.wait()


def second_kernel(
    small_qkv, small_grad, ids_hbm, before, kept_before, given_before, small_out, kept_hbm, given_hbm, *scratch
):
    @pl.when(lax.axis_index("dp") % 2 == 0)
    def _():
        loads = small_loads(small_qkv, small_grad, ids_hbm, scratch)
        for load in loads:
            load.start()
        small_images(loads, small_out, kept_hbm, given_hbm, 0, HEADS, scratch)


def pieces(row):
    high = row.astype(BF16).astype(F32)
    return jnp.concatenate([high, (row - high).astype(BF16).astype(F32)], axis=0)


def big_kernel(in_ref, sums_ref, out_ref, feat):
    pairs = in_ref.shape[0] // 2
    half = LANES // 2
    for pair in range(pairs):
        one, two = in_ref[2 * pair], in_ref[2 * pair + 1]
        columns = slice(LANES * pair, LANES * (pair + 1))
        feat[:IN_ROWS, columns] = jnp.concatenate([one[:, :half], two[:, :half]], axis=1)
        feat[IN_ROWS:, columns] = jnp.concatenate([one[:, half:], two[:, half:]], axis=1)
    query, key, value, grad = (feat[HEAD * which : HEAD * (which + 1)] for which in range(4))
    length = key.shape[1]
    weights, slopes = slopes_of(dot(key.T, query, 1, 0), dot(value.T, grad, 1, 0))
    query_grad = (dot(key, slopes, 1, 0) * SCALE).astype(BF16)
    key_grad = dot(query, slopes, 1, 1) * SCALE
    value_grad = dot(grad, weights, 1, 1)
    big_row = dot(jnp.ones((8, length), BF16), query_grad, 1, 1)[:1]
    big_row = jnp.concatenate([big_row, jnp.zeros((1, LANES - HEAD), F32)], axis=1)
    extra = pieces(jnp.concatenate([sums_ref[...], big_row], axis=0))
    whole = jnp.concatenate([query_grad.astype(F32), key_grad, value_grad], axis=0)
    for pair in range(pairs):
        block = whole[:, LANES * pair : LANES * (pair + 1)]
        upper, lower = block[:OUT_ROWS], block[OUT_ROWS:]
        one = jnp.concatenate([upper[:, :half], lower[:, :half]], axis=1)
        two = jnp.concatenate([upper[:, half:], lower[:, half:]], axis=1)
        out_ref[2 * pair] = jnp.concatenate([one, extra], axis=0).astype(BF16)
        out_ref[2 * pair + 1] = jnp.concatenate([two, extra], axis=0).astype(BF16)


def unpack_kernel(in_ref, out_ref):
    half = LANES // 2
    parts = []
    for head in range(HEADS):
        block = in_ref[head].astype(F32)[:OUT_ROWS]
        parts.append(jnp.concatenate([block[:, :half], block[:, half:]], axis=0).astype(BF16))
    out_ref[...] = jnp.concatenate(parts, axis=0).T


def call(kernel, shapes, in_specs, out_specs, operands, scratch=(), mebibytes=60, flops=0, name=None, aliases=None):
    return pl.pallas_call(
        kernel,
        out_shape=shapes,
        in_specs=in_specs,
        out_specs=out_specs,
        scratch_shapes=scratch,
        compiler_params=params(mebibytes),
        cost_estimate=pl.CostEstimate(flops=flops, bytes_accessed=2**20, transcendentals=0),
        input_output_aliases=aliases or {},
        name=name,
    )(*operands)


VMEM = pl.BlockSpec(memory_space=pltpu.VMEM)
ANY = pl.BlockSpec(memory_space=pl.ANY)


def halved(given, images, step, cores):
    pairs = [(at, at ^ STEPS[at % 2][step][0]) for at in range(images) if at % 2 in cores]
    return lax.ppermute(given, "dp", pairs)


def local(big_qkv, big_grad, small_qkv, small_grad, small_ids):
    rows = big_qkv.shape[0]
    small_rows = small_qkv.shape[0]
    images = lax.axis_size("dp")
    parts = lax.axis_size("seq")
    length = rows * parts
    ring = [[(at + FIRST_PART) % parts for at in range(parts)]]
    plane = [[(at + FIRST_IMAGE) % images for at in range(images)]]
    width = 3 * HEAD * HEADS
    image = lax.axis_index("dp")

    small_scratch = [
        pltpu.VMEM((small_rows, width), BF16),
        pltpu.VMEM((small_rows, HEAD * HEADS), BF16),
        pltpu.VMEM((1, small_rows), jnp.int32),
        pltpu.VMEM((width, small_rows), BF16),
        pltpu.VMEM((HEAD * HEADS, small_rows), BF16),
        pltpu.VMEM((width, small_rows), BF16),
        pltpu.VMEM((small_rows, width), BF16),
        pltpu.VMEM((HEAD * HEADS, small_rows), BF16),
        pltpu.VMEM((1, HEAD * HEADS // 2), F32),
        pltpu.VMEM((1, HEAD * HEADS // 2), F32),
        pltpu.SemaphoreType.DMA((3,)),
    ]
    small_shape = jax.ShapeDtypeStruct((small_rows, width), BF16)
    sum_shapes = [jax.ShapeDtypeStruct((1, HEADS * HEAD // 2), F32)] * 2
    sent, small_out, *sums = call(
        first_kernel,
        [jax.ShapeDtypeStruct((HEADS, IN_ROWS, LANES), BF16), small_shape, *sum_shapes],
        [ANY] * 5,
        [ANY] * 4,
        (big_qkv, big_grad, small_qkv, small_grad, small_ids),
        [
            pltpu.VMEM((rows, width), BF16),
            pltpu.VMEM((rows, HEAD * HEADS), BF16),
            pltpu.VMEM((HEADS, IN_ROWS, LANES), BF16),
            pltpu.SemaphoreType.DMA((2, 2)),
            pltpu.SemaphoreType.DMA((2,)),
            *small_scratch,
        ],
        name="pack",
    )
    late = halved(sums[1], images, 0, (1,))
    sent, late = lax.optimization_barrier((sent, late))
    got = lax.all_to_all(sent, "seq", 0, 0, axis_index_groups=ring, tiled=True)

    small_out, *sums = call(
        second_kernel,
        [small_shape, *sum_shapes],
        [ANY] * 6,
        [ANY] * 3,
        (small_qkv, small_grad, small_ids, small_out, *sums),
        small_scratch,
        flops=10**10,
        name="small",
        aliases={3: 0, 4: 1, 5: 2},
    )

    early = halved(sums[1], images, 0, (0,))
    sums = (sums[0] + late + early).reshape(2 * SHARE)
    upper = jnp.where(image % 2 == 0, *[image // STEPS[core][1][1] % 2 for core in range(2)])
    kept = lax.dynamic_slice(sums, (upper * SHARE,), (SHARE,))
    given = lax.dynamic_slice(sums, ((1 - upper) * SHARE,), (SHARE,))
    sums = kept + halved(given, images, 1, (0, 1))
    sums = jnp.pad(sums, (0, 3 * LANES - SHARE)).reshape(3, LANES)

    back = call(
        big_kernel,
        jax.ShapeDtypeStruct((parts, OUT_ROWS + SUM_ROWS, LANES), BF16),
        [VMEM, VMEM],
        VMEM,
        (got, sums),
        mebibytes=40,
        scratch=[pltpu.VMEM((4 * HEAD, length), BF16)],
        flops=10**10,
        name="big",
    )
    home = lax.all_to_all(back, "seq", 0, 0, axis_index_groups=ring, tiled=True)

    extra = home[:, OUT_ROWS:].astype(F32)
    extra = extra[:, :4] + extra[:, 4:]
    share = jnp.sum(extra[:, :3], axis=0).reshape(3 * LANES)[:SHARE]
    quarters = [image // first % 2 * 2 + image // second % 2 for (_, first), (_, second) in STEPS]
    held = jnp.arange(4) == jnp.where(image % 2 == 0, *quarters)
    total = extra[:, 3, :HEAD].reshape(HEADS * HEAD) + jnp.where(held[:, None], share, 0.0).reshape(HEADS * HEAD)
    everyone = lax.all_to_all(
        jnp.broadcast_to(total, (images, 1, HEADS * HEAD)), "dp", 0, 0, axis_index_groups=plane, tiled=True
    )
    bias_grad = jnp.sum(everyone, axis=(0, 1))

    big_out = call(
        unpack_kernel,
        jax.ShapeDtypeStruct((rows, width), BF16),
        [VMEM],
        VMEM,
        (home,),
        mebibytes=8,
        flops=10**9,
        name="unpack",
    )
    return big_out, small_out, bias_grad


def solution(mesh):
    spec = P(("dp", "seq"), None)
    return jax.shard_map(
        local,
        mesh=mesh,
        in_specs=(spec,) * 5,
        out_specs=(spec, spec, P()),
        check_vma=False,
    )
```

```python
import math

import jax
import jax.numpy as jnp
from jax import lax
from jax.experimental import pallas as pl
from jax.experimental.pallas import tpu as pltpu
from jax.sharding import PartitionSpec as P

HEAD = 80
HEADS = 16
SCALE = HEAD ** (-0.5)
LANES = 128
FIRST_PART = 10
FIRST_IMAGE = 21
TOGETHER = 1
IN_ROWS = 2 * HEAD
OUT_ROWS = 3 * HEAD // 2
SUM_ROWS = 8
STEPS = (((2, 2), (8, 8)), ((20, 4), (2, 2)))
SHARE = HEADS * HEAD // 4
EXPONENT = SCALE * math.log2(math.e)
F32 = jnp.float32
BF16 = jnp.bfloat16


def dot(left, right, left_dim, right_dim):
    return lax.dot_general(
        left, right, (((left_dim,), (right_dim,)), ((), ())), preferred_element_type=F32
    )


def params(mebibytes):
    return pltpu.CompilerParams(vmem_limit_bytes=mebibytes * 1024 * 1024)


def slopes_of(scores, upstream):
    exponent = jnp.exp2((scores - jnp.max(scores, axis=0, keepdims=True)) * EXPONENT)
    inverse = 1.0 / jnp.sum(exponent, axis=0, keepdims=True)
    delta = jnp.sum(exponent * upstream, axis=0, keepdims=True) * inverse
    probs = exponent * inverse
    return probs.astype(BF16), (probs * (upstream - delta)).astype(BF16)


def small_loads(qkv_hbm, grad_hbm, ids_hbm, scratch):
    sems = scratch[-1]
    sources = (qkv_hbm, grad_hbm, ids_hbm)
    return [pltpu.make_async_copy(sources[at], scratch[at], sems.at[at]) for at in range(3)]


def small_images(loads, out_hbm, kept_hbm, given_hbm, core, together, scratch):
    qkv, grads, ids_ref, qkv_t, grad_t, out_t, out, query_t, kept, given, sems = scratch
    rows = qkv.shape[0]
    for load in loads:
        load.wait()
    ids = jnp.broadcast_to(ids_ref[...].astype(F32), (rows, rows))
    allowed = ids == ids.T
    qkv_t[...] = qkv[...].T
    grad_t[...] = grads[...].T

    def place(head, which=0, count=3):
        first = count * HEAD * head + HEAD * which
        return pl.ds(first if isinstance(first, int) else pl.multiple_of(first, 16), HEAD)

    def some(heads):
        query, key, value = ([qkv_t[place(head, which)] for head in heads] for which in range(3))
        grad = [grad_t[place(head, 0, 1)] for head in heads]
        scores = [jnp.where(allowed, dot(*pair, 0, 0), -1e30) for pair in zip(key, query)]
        upstream = [dot(*pair, 0, 0) for pair in zip(value, grad)]
        weights, slopes = zip(*[slopes_of(*pair) for pair in zip(scores, upstream)])
        query_grad = [(dot(*pair, 1, 0) * SCALE).astype(BF16) for pair in zip(key, slopes)]
        key_grad = [(dot(*pair, 1, 1) * SCALE).astype(BF16) for pair in zip(query, slopes)]
        value_grad = [dot(*pair, 1, 1).astype(BF16) for pair in zip(grad, weights)]
        for at, head in enumerate(heads):
            query_t[place(head, 0, 1)] = query_grad[at]
            for which, result in enumerate((query_grad, key_grad, value_grad)):
                out_t[place(head, which)] = result[at]

    if together == HEADS:
        some(range(HEADS))
    else:

        @pl.loop(0, HEADS // together)
        def _(step):
            some([step * together + at for at in range(together)])

    sums = dot(jnp.ones((8, rows), BF16), query_t[...], 1, 1)[:1]
    half = HEADS * HEAD // 2
    upper = lax.axis_index("dp") // STEPS[core][0][1] % 2
    kept[...] = jnp.where(upper == 1, sums[:, half:], sums[:, :half])
    given[...] = jnp.where(upper == 1, sums[:, :half], sums[:, half:])
    out[...] = out_t[...].T
    stores = [
        pltpu.make_async_copy(out, out_hbm, sems.at[0]),
        pltpu.make_async_copy(kept, kept_hbm, sems.at[1]),
        pltpu.make_async_copy(given, given_hbm, sems.at[2]),
    ]
    for store in stores:
        store.start()
    for store in stores:
        store.wait()


def first_kernel(
    qkv_hbm,
    grad_hbm,
    small_qkv,
    small_grad,
    ids_hbm,
    out_hbm,
    small_out,
    kept_hbm,
    given_hbm,
    qkv,
    grad,
    packed,
    in_sems,
    out_sems,
    *scratch,
):
    parts = in_sems.shape[1]
    heads = HEADS // parts
    wide, narrow = 3 * HEAD * heads, HEAD * heads
    loads = []
    for part in range(parts):
        columns = pl.ds(part * wide, wide)
        loads.append(
            pltpu.make_async_copy(qkv_hbm.at[:, columns], qkv.at[:, columns], in_sems.at[0, part])
        )
        columns = pl.ds(part * narrow, narrow)
        loads.append(
            pltpu.make_async_copy(grad_hbm.at[:, columns], grad.at[:, columns], in_sems.at[1, part])
        )
    for load in loads:
        load.start()
    late = lax.axis_index("dp") % 2 == 1
    after = small_loads(small_qkv, small_grad, ids_hbm, scratch)

    @pl.when(late)
    def _():
        for load in after:
            load.start()

    stores = []
    for part in range(parts):
        loads[2 * part].wait()
        loads[2 * part + 1].wait()
        turned = qkv[:, part * wide : (part + 1) * wide].T
        turned_grad = grad[:, part * narrow : (part + 1) * narrow].T
        for index in range(heads):
            first = 3 * HEAD * index
            left = turned[first : first + 2 * HEAD]
            right = jnp.concatenate(
                [
                    turned[first + 2 * HEAD : first + 3 * HEAD],
                    turned_grad[HEAD * index : HEAD * (index + 1)],
                ],
                axis=0,
            )
            packed[part * heads + index] = jnp.concatenate([left, right], axis=1)
        done = pl.ds(part * heads, heads)
        stores.append(pltpu.make_async_copy(packed.at[done], out_hbm.at[done], out_sems.at[part]))
        stores[-1].start()

    @pl.when(late)
    def _():
        small_images(after, small_out, kept_hbm, given_hbm, 1, TOGETHER, scratch)

    for store in stores:
        store.wait()


def second_kernel(
    small_qkv, small_grad, ids_hbm, before, kept_before, given_before, small_out, kept_hbm, given_hbm, *scratch
):
    @pl.when(lax.axis_index("dp") % 2 == 0)
    def _():
        loads = small_loads(small_qkv, small_grad, ids_hbm, scratch)
        for load in loads:
            load.start()
        small_images(loads, small_out, kept_hbm, given_hbm, 0, HEADS, scratch)


def pieces(row):
    high = row.astype(BF16).astype(F32)
    return jnp.concatenate([high, (row - high).astype(BF16).astype(F32)], axis=0)


def big_kernel(in_ref, sums_ref, out_ref, feat):
    pairs = in_ref.shape[0] // 2
    half = LANES // 2
    for pair in range(pairs):
        one, two = in_ref[2 * pair], in_ref[2 * pair + 1]
        columns = slice(LANES * pair, LANES * (pair + 1))
        feat[:IN_ROWS, columns] = jnp.concatenate([one[:, :half], two[:, :half]], axis=1)
        feat[IN_ROWS:, columns] = jnp.concatenate([one[:, half:], two[:, half:]], axis=1)
    query, key, value, grad = (feat[HEAD * which : HEAD * (which + 1)] for which in range(4))
    length = key.shape[1]
    weights, slopes = slopes_of(dot(key.T, query, 1, 0), dot(value.T, grad, 1, 0))
    query_grad = (dot(key, slopes, 1, 0) * SCALE).astype(BF16)
    key_grad = dot(query, slopes, 1, 1) * SCALE
    value_grad = dot(grad, weights, 1, 1)
    big_row = dot(jnp.ones((8, length), BF16), query_grad, 1, 1)[:1]
    big_row = jnp.concatenate([big_row, jnp.zeros((1, LANES - HEAD), F32)], axis=1)
    extra = pieces(jnp.concatenate([sums_ref[...], big_row], axis=0))
    whole = jnp.concatenate([query_grad.astype(F32), key_grad, value_grad], axis=0)
    for pair in range(pairs):
        block = whole[:, LANES * pair : LANES * (pair + 1)]
        upper, lower = block[:OUT_ROWS], block[OUT_ROWS:]
        one = jnp.concatenate([upper[:, :half], lower[:, :half]], axis=1)
        two = jnp.concatenate([upper[:, half:], lower[:, half:]], axis=1)
        out_ref[2 * pair] = jnp.concatenate([one, extra], axis=0).astype(BF16)
        out_ref[2 * pair + 1] = jnp.concatenate([two, extra], axis=0).astype(BF16)


def spread_kernel(in_ref, out_ref):
    image = lax.axis_index("dp")
    quarters = [image // first % 2 * 2 + image // second % 2 for (_, first), (_, second) in STEPS]
    quarter = jnp.where(image % 2 == 0, *quarters)
    sums = in_ref[:, OUT_ROWS:].astype(F32)
    sums = sums[:, : SUM_ROWS // 2] + sums[:, SUM_ROWS // 2 :]
    share = jnp.sum(sums[:, :3], axis=0)
    share = jnp.concatenate([share[at : at + 1] for at in range(3)], axis=1)[:, :SHARE]
    columns = lax.broadcasted_iota(jnp.int32, (1, HEADS * HEAD), 1) - quarter * SHARE
    share = jnp.concatenate([share] * 4, axis=1)
    big = jnp.concatenate([sums[head, 3:, :HEAD] for head in range(HEADS)], axis=1)
    total = big + jnp.where((columns >= 0) & (columns < SHARE), share, 0.0)
    out_ref[...] = jnp.broadcast_to(total[None], out_ref.shape)


def unpack_kernel(in_ref, out_ref):
    half = LANES // 2
    parts = []
    for head in range(HEADS):
        block = in_ref[head].astype(F32)[:OUT_ROWS]
        parts.append(jnp.concatenate([block[:, :half], block[:, half:]], axis=0).astype(BF16))
    out_ref[...] = jnp.concatenate(parts, axis=0).T


def call(kernel, shapes, in_specs, out_specs, operands, scratch=(), mebibytes=60, flops=0, name=None, aliases=None):
    return pl.pallas_call(
        kernel,
        out_shape=shapes,
        in_specs=in_specs,
        out_specs=out_specs,
        scratch_shapes=scratch,
        compiler_params=params(mebibytes),
        cost_estimate=pl.CostEstimate(flops=flops, bytes_accessed=2**20, transcendentals=0),
        input_output_aliases=aliases or {},
        name=name,
    )(*operands)


VMEM = pl.BlockSpec(memory_space=pltpu.VMEM)
ANY = pl.BlockSpec(memory_space=pl.ANY)


def halved(given, images, step, cores):
    pairs = [(at, at ^ STEPS[at % 2][step][0]) for at in range(images) if at % 2 in cores]
    return lax.ppermute(given, "dp", pairs)


def local(big_qkv, big_grad, small_qkv, small_grad, small_ids):
    rows = big_qkv.shape[0]
    small_rows = small_qkv.shape[0]
    images = lax.axis_size("dp")
    parts = lax.axis_size("seq")
    length = rows * parts
    ring = [[(at + FIRST_PART) % parts for at in range(parts)]]
    plane = [[(at + FIRST_IMAGE) % images for at in range(images)]]
    width = 3 * HEAD * HEADS
    image = lax.axis_index("dp")

    small_scratch = [
        pltpu.VMEM((small_rows, width), BF16),
        pltpu.VMEM((small_rows, HEAD * HEADS), BF16),
        pltpu.VMEM((1, small_rows), jnp.int32),
        pltpu.VMEM((width, small_rows), BF16),
        pltpu.VMEM((HEAD * HEADS, small_rows), BF16),
        pltpu.VMEM((width, small_rows), BF16),
        pltpu.VMEM((small_rows, width), BF16),
        pltpu.VMEM((HEAD * HEADS, small_rows), BF16),
        pltpu.VMEM((1, HEAD * HEADS // 2), F32),
        pltpu.VMEM((1, HEAD * HEADS // 2), F32),
        pltpu.SemaphoreType.DMA((3,)),
    ]
    small_shape = jax.ShapeDtypeStruct((small_rows, width), BF16)
    sum_shapes = [jax.ShapeDtypeStruct((1, HEADS * HEAD // 2), F32)] * 2
    sent, small_out, *sums = call(
        first_kernel,
        [jax.ShapeDtypeStruct((HEADS, IN_ROWS, LANES), BF16), small_shape, *sum_shapes],
        [ANY] * 5,
        [ANY] * 4,
        (big_qkv, big_grad, small_qkv, small_grad, small_ids),
        [
            pltpu.VMEM((rows, width), BF16),
            pltpu.VMEM((rows, HEAD * HEADS), BF16),
            pltpu.VMEM((HEADS, IN_ROWS, LANES), BF16),
            pltpu.SemaphoreType.DMA((2, 2)),
            pltpu.SemaphoreType.DMA((2,)),
            *small_scratch,
        ],
        name="pack",
    )
    late = halved(sums[1], images, 0, (1,))
    sent, late = lax.optimization_barrier((sent, late))
    got = lax.all_to_all(sent, "seq", 0, 0, axis_index_groups=ring, tiled=True)

    small_out, *sums = call(
        second_kernel,
        [small_shape, *sum_shapes],
        [ANY] * 6,
        [ANY] * 3,
        (small_qkv, small_grad, small_ids, small_out, *sums),
        small_scratch,
        flops=10**10,
        name="small",
        aliases={3: 0, 4: 1, 5: 2},
    )

    early = halved(sums[1], images, 0, (0,))
    sums = (sums[0] + late + early).reshape(2 * SHARE)
    upper = jnp.where(image % 2 == 0, *[image // STEPS[core][1][1] % 2 for core in range(2)])
    kept = lax.dynamic_slice(sums, (upper * SHARE,), (SHARE,))
    given = lax.dynamic_slice(sums, ((1 - upper) * SHARE,), (SHARE,))
    sums = kept + halved(given, images, 1, (0, 1))
    sums = jnp.pad(sums, (0, 3 * LANES - SHARE)).reshape(3, LANES)

    back = call(
        big_kernel,
        jax.ShapeDtypeStruct((parts, OUT_ROWS + SUM_ROWS, LANES), BF16),
        [VMEM, VMEM],
        VMEM,
        (got, sums),
        mebibytes=40,
        scratch=[pltpu.VMEM((4 * HEAD, length), BF16)],
        flops=10**10,
        name="big",
    )
    home = lax.all_to_all(back, "seq", 0, 0, axis_index_groups=ring, tiled=True)

    total = call(
        spread_kernel,
        jax.ShapeDtypeStruct((images, 1, HEADS * HEAD), F32),
        [VMEM],
        VMEM,
        (home,),
        mebibytes=8,
        name="spread",
    )
    everyone = lax.all_to_all(total, "dp", 0, 0, axis_index_groups=plane, tiled=True)
    bias_grad = jnp.sum(everyone, axis=(0, 1))

    big_out = call(
        unpack_kernel,
        jax.ShapeDtypeStruct((rows, width), BF16),
        [VMEM],
        VMEM,
        (home,),
        mebibytes=8,
        flops=10**9,
        name="unpack",
    )
    return big_out, small_out, bias_grad


def solution(mesh):
    spec = P(("dp", "seq"), None)
    return jax.shard_map(
        local,
        mesh=mesh,
        in_specs=(spec,) * 5,
        out_specs=(spec, spec, P()),
        check_vma=False,
    )
```

```python
import math

import jax
import jax.numpy as jnp
from jax import lax
from jax.experimental import pallas as pl
from jax.experimental.pallas import tpu as pltpu
from jax.sharding import PartitionSpec as P

HEAD = 80
HEADS = 16
SCALE = HEAD ** (-0.5)
LANES = 128
FIRST_PART = 10
FIRST_IMAGE = 21
TOGETHER = 1
IN_ROWS = 2 * HEAD
OUT_ROWS = 3 * HEAD // 2
SUM_ROWS = 8
STEPS = (((2, 2), (8, 8)), ((20, 4), (2, 2)))
SHARE = HEADS * HEAD // 4
EXPONENT = SCALE * math.log2(math.e)
F32 = jnp.float32
BF16 = jnp.bfloat16


def dot(left, right, left_dim, right_dim):
    return lax.dot_general(
        left, right, (((left_dim,), (right_dim,)), ((), ())), preferred_element_type=F32
    )


def params(mebibytes):
    return pltpu.CompilerParams(vmem_limit_bytes=mebibytes * 1024 * 1024)


def slopes_of(scores, upstream):
    exponent = jnp.exp2((scores - jnp.max(scores, axis=0, keepdims=True)) * EXPONENT)
    inverse = 1.0 / jnp.sum(exponent, axis=0, keepdims=True)
    delta = jnp.sum(exponent * upstream, axis=0, keepdims=True) * inverse
    probs = exponent * inverse
    return probs.astype(BF16), (probs * (upstream - delta)).astype(BF16)


def small_loads(qkv_hbm, grad_hbm, ids_hbm, scratch):
    sems = scratch[-1]
    sources = (qkv_hbm, grad_hbm, ids_hbm)
    return [pltpu.make_async_copy(sources[at], scratch[at], sems.at[at]) for at in range(3)]


def small_images(loads, out_hbm, kept_hbm, given_hbm, core, together, scratch):
    qkv, grads, ids_ref, qkv_t, grad_t, out_t, out, query_t, kept, given, sems = scratch
    rows = qkv.shape[0]
    for load in loads:
        load.wait()
    ids = jnp.broadcast_to(ids_ref[...].astype(F32), (rows, rows))
    allowed = ids == ids.T
    qkv_t[...] = qkv[...].T
    grad_t[...] = grads[...].T

    def place(head, which=0, count=3):
        first = count * HEAD * head + HEAD * which
        return pl.ds(first if isinstance(first, int) else pl.multiple_of(first, 16), HEAD)

    def some(heads):
        query, key, value = ([qkv_t[place(head, which)] for head in heads] for which in range(3))
        grad = [grad_t[place(head, 0, 1)] for head in heads]
        scores = [jnp.where(allowed, dot(*pair, 0, 0), -1e30) for pair in zip(key, query)]
        upstream = [dot(*pair, 0, 0) for pair in zip(value, grad)]
        weights, slopes = zip(*[slopes_of(*pair) for pair in zip(scores, upstream)])
        query_grad = [(dot(*pair, 1, 0) * SCALE).astype(BF16) for pair in zip(key, slopes)]
        key_grad = [(dot(*pair, 1, 1) * SCALE).astype(BF16) for pair in zip(query, slopes)]
        value_grad = [dot(*pair, 1, 1).astype(BF16) for pair in zip(grad, weights)]
        for at, head in enumerate(heads):
            query_t[place(head, 0, 1)] = query_grad[at]
            for which, result in enumerate((query_grad, key_grad, value_grad)):
                out_t[place(head, which)] = result[at]

    if together == HEADS:
        some(range(HEADS))
    else:

        @pl.loop(0, HEADS // together)
        def _(step):
            some([step * together + at for at in range(together)])

    sums = dot(jnp.ones((8, rows), BF16), query_t[...], 1, 1)[:1]
    half = HEADS * HEAD // 2
    upper = lax.axis_index("dp") // STEPS[core][0][1] % 2
    kept[...] = jnp.where(upper == 1, sums[:, half:], sums[:, :half])
    given[...] = jnp.where(upper == 1, sums[:, :half], sums[:, half:])
    out[...] = out_t[...].T
    stores = [
        pltpu.make_async_copy(out, out_hbm, sems.at[0]),
        pltpu.make_async_copy(kept, kept_hbm, sems.at[1]),
        pltpu.make_async_copy(given, given_hbm, sems.at[2]),
    ]
    for store in stores:
        store.start()
    for store in stores:
        store.wait()


def first_kernel(
    qkv_hbm,
    grad_hbm,
    small_qkv,
    small_grad,
    ids_hbm,
    out_hbm,
    small_out,
    kept_hbm,
    given_hbm,
    qkv,
    grad,
    packed,
    in_sems,
    out_sems,
    *scratch,
):
    parts = in_sems.shape[1]
    heads = HEADS // parts
    wide, narrow = 3 * HEAD * heads, HEAD * heads
    loads = []
    for part in range(parts):
        columns = pl.ds(part * wide, wide)
        loads.append(
            pltpu.make_async_copy(qkv_hbm.at[:, columns], qkv.at[:, columns], in_sems.at[0, part])
        )
        columns = pl.ds(part * narrow, narrow)
        loads.append(
            pltpu.make_async_copy(grad_hbm.at[:, columns], grad.at[:, columns], in_sems.at[1, part])
        )
    for load in loads:
        load.start()
    late = lax.axis_index("dp") % 2 == 1
    after = small_loads(small_qkv, small_grad, ids_hbm, scratch)

    @pl.when(late)
    def _():
        for load in after:
            load.start()

    stores = []
    for part in range(parts):
        loads[2 * part].wait()
        loads[2 * part + 1].wait()
        turned = qkv[:, part * wide : (part + 1) * wide].T
        turned_grad = grad[:, part * narrow : (part + 1) * narrow].T
        for index in range(heads):
            first = 3 * HEAD * index
            left = turned[first : first + 2 * HEAD]
            right = jnp.concatenate(
                [
                    turned[first + 2 * HEAD : first + 3 * HEAD],
                    turned_grad[HEAD * index : HEAD * (index + 1)],
                ],
                axis=0,
            )
            packed[part * heads + index] = jnp.concatenate([left, right], axis=1)
        done = pl.ds(part * heads, heads)
        stores.append(pltpu.make_async_copy(packed.at[done], out_hbm.at[done], out_sems.at[part]))
        stores[-1].start()

    @pl.when(late)
    def _():
        small_images(after, small_out, kept_hbm, given_hbm, 1, TOGETHER, scratch)

    for store in stores:
        store.wait()


def second_kernel(
    small_qkv, small_grad, ids_hbm, before, kept_before, given_before, small_out, kept_hbm, given_hbm, *scratch
):
    @pl.when(lax.axis_index("dp") % 2 == 0)
    def _():
        loads = small_loads(small_qkv, small_grad, ids_hbm, scratch)
        for load in loads:
            load.start()
        small_images(loads, small_out, kept_hbm, given_hbm, 0, HEADS, scratch)


def pieces(row):
    high = row.astype(BF16).astype(F32)
    return jnp.concatenate([high, (row - high).astype(BF16).astype(F32)], axis=0)


def big_kernel(in_ref, sums_ref, out_ref, feat):
    pairs = in_ref.shape[0] // 2
    half = LANES // 2
    for pair in range(pairs):
        one, two = in_ref[2 * pair], in_ref[2 * pair + 1]
        columns = slice(LANES * pair, LANES * (pair + 1))
        feat[:IN_ROWS, columns] = jnp.concatenate([one[:, :half], two[:, :half]], axis=1)
        feat[IN_ROWS:, columns] = jnp.concatenate([one[:, half:], two[:, half:]], axis=1)
    query, key, value, grad = (feat[HEAD * which : HEAD * (which + 1)] for which in range(4))
    length = key.shape[1]
    weights, slopes = slopes_of(dot(key.T, query, 1, 0), dot(value.T, grad, 1, 0))
    query_grad = (dot(key, slopes, 1, 0) * SCALE).astype(BF16)
    key_grad = dot(query, slopes, 1, 1) * SCALE
    value_grad = dot(grad, weights, 1, 1)
    big_row = dot(jnp.ones((8, length), BF16), query_grad, 1, 1)[:1]
    big_row = jnp.concatenate([big_row, jnp.zeros((1, LANES - HEAD), F32)], axis=1)
    extra = pieces(jnp.concatenate([sums_ref[...], big_row], axis=0))
    whole = jnp.concatenate([query_grad.astype(F32), key_grad, value_grad], axis=0)
    for pair in range(pairs):
        block = whole[:, LANES * pair : LANES * (pair + 1)]
        upper, lower = block[:OUT_ROWS], block[OUT_ROWS:]
        one = jnp.concatenate([upper[:, :half], lower[:, :half]], axis=1)
        two = jnp.concatenate([upper[:, half:], lower[:, half:]], axis=1)
        out_ref[2 * pair] = jnp.concatenate([one, extra], axis=0).astype(BF16)
        out_ref[2 * pair + 1] = jnp.concatenate([two, extra], axis=0).astype(BF16)


def spread_kernel(in_ref, out_ref):
    image = lax.axis_index("dp")
    quarters = [image // first % 2 * 2 + image // second % 2 for (_, first), (_, second) in STEPS]
    quarter = jnp.where(image % 2 == 0, *quarters)
    sums = in_ref[:, OUT_ROWS:].astype(F32)
    sums = sums[:, : SUM_ROWS // 2] + sums[:, SUM_ROWS // 2 :]
    share = jnp.sum(sums[:, :3], axis=0)
    share = jnp.concatenate([share[at : at + 1] for at in range(3)], axis=1)[:, :SHARE]
    columns = lax.broadcasted_iota(jnp.int32, (1, HEADS * HEAD), 1) - quarter * SHARE
    share = jnp.concatenate([share] * 4, axis=1)
    big = jnp.concatenate([sums[head, 3:, :HEAD] for head in range(HEADS)], axis=1)
    total = big + jnp.where((columns >= 0) & (columns < SHARE), share, 0.0)
    out_ref[...] = jnp.broadcast_to(total[None], out_ref.shape)


def unpack_kernel(in_ref, out_ref):
    half = LANES // 2
    parts = []
    for head in range(HEADS):
        block = in_ref[head].astype(F32)[:OUT_ROWS]
        parts.append(jnp.concatenate([block[:, :half], block[:, half:]], axis=0).astype(BF16))
    out_ref[...] = jnp.concatenate(parts, axis=0).T


def call(kernel, shapes, in_specs, out_specs, operands, scratch=(), mebibytes=60, flops=0, name=None, aliases=None):
    return pl.pallas_call(
        kernel,
        out_shape=shapes,
        in_specs=in_specs,
        out_specs=out_specs,
        scratch_shapes=scratch,
        compiler_params=params(mebibytes),
        cost_estimate=pl.CostEstimate(flops=flops, bytes_accessed=2**20, transcendentals=0),
        input_output_aliases=aliases or {},
        name=name,
    )(*operands)


VMEM = pl.BlockSpec(memory_space=pltpu.VMEM)
ANY = pl.BlockSpec(memory_space=pl.ANY)


def halved(given, images, step, cores):
    pairs = [(at, at ^ STEPS[at % 2][step][0]) for at in range(images) if at % 2 in cores]
    return lax.ppermute(given, "dp", pairs)


def local(big_qkv, big_grad, small_qkv, small_grad, small_ids):
    rows = big_qkv.shape[0]
    small_rows = small_qkv.shape[0]
    images = lax.axis_size("dp")
    parts = lax.axis_size("seq")
    length = rows * parts
    ring = [[(at + FIRST_PART) % parts for at in range(parts)]]
    plane = [[(at + FIRST_IMAGE) % images for at in range(images)]]
    width = 3 * HEAD * HEADS
    image = lax.axis_index("dp")

    small_scratch = [
        pltpu.VMEM((small_rows, width), BF16),
        pltpu.VMEM((small_rows, HEAD * HEADS), BF16),
        pltpu.VMEM((1, small_rows), jnp.int32),
        pltpu.VMEM((width, small_rows), BF16),
        pltpu.VMEM((HEAD * HEADS, small_rows), BF16),
        pltpu.VMEM((width, small_rows), BF16),
        pltpu.VMEM((small_rows, width), BF16),
        pltpu.VMEM((HEAD * HEADS, small_rows), BF16),
        pltpu.VMEM((1, HEAD * HEADS // 2), F32),
        pltpu.VMEM((1, HEAD * HEADS // 2), F32),
        pltpu.SemaphoreType.DMA((3,)),
    ]
    small_shape = jax.ShapeDtypeStruct((small_rows, width), BF16)
    sum_shapes = [jax.ShapeDtypeStruct((1, HEADS * HEAD // 2), F32)] * 2
    sent, small_out, *sums = call(
        first_kernel,
        [jax.ShapeDtypeStruct((HEADS, IN_ROWS, LANES), BF16), small_shape, *sum_shapes],
        [ANY] * 5,
        [ANY] * 4,
        (big_qkv, big_grad, small_qkv, small_grad, small_ids),
        [
            pltpu.VMEM((rows, width), BF16),
            pltpu.VMEM((rows, HEAD * HEADS), BF16),
            pltpu.VMEM((HEADS, IN_ROWS, LANES), BF16),
            pltpu.SemaphoreType.DMA((2, 2)),
            pltpu.SemaphoreType.DMA((2,)),
            *small_scratch,
        ],
        name="pack",
    )
    late = lax.cond(
        image % 2 == 1, lambda given: halved(given, images, 0, (1,)), lambda given: given, sums[1]
    )
    sent, late = lax.optimization_barrier((sent, late))
    got = lax.all_to_all(sent, "seq", 0, 0, axis_index_groups=ring, tiled=True)

    small_out, *sums = call(
        second_kernel,
        [small_shape, *sum_shapes],
        [ANY] * 6,
        [ANY] * 3,
        (small_qkv, small_grad, small_ids, small_out, *sums),
        small_scratch,
        flops=10**10,
        name="small",
        aliases={3: 0, 4: 1, 5: 2},
    )

    early = halved(sums[1], images, 0, (0,))
    sums = (sums[0] + jnp.where(image % 2 == 1, late, early)).reshape(2 * SHARE)
    upper = jnp.where(image % 2 == 0, *[image // STEPS[core][1][1] % 2 for core in range(2)])
    kept = lax.dynamic_slice(sums, (upper * SHARE,), (SHARE,))
    given = lax.dynamic_slice(sums, ((1 - upper) * SHARE,), (SHARE,))
    sums = kept + halved(given, images, 1, (0, 1))
    sums = jnp.pad(sums, (0, 3 * LANES - SHARE)).reshape(3, LANES)

    back = call(
        big_kernel,
        jax.ShapeDtypeStruct((parts, OUT_ROWS + SUM_ROWS, LANES), BF16),
        [VMEM, VMEM],
        VMEM,
        (got, sums),
        mebibytes=40,
        scratch=[pltpu.VMEM((4 * HEAD, length), BF16)],
        flops=10**10,
        name="big",
    )
    home = lax.all_to_all(back, "seq", 0, 0, axis_index_groups=ring, tiled=True)

    total = call(
        spread_kernel,
        jax.ShapeDtypeStruct((images, 1, HEADS * HEAD), F32),
        [VMEM],
        VMEM,
        (home,),
        mebibytes=8,
        name="spread",
    )
    everyone = lax.all_to_all(total, "dp", 0, 0, axis_index_groups=plane, tiled=True)
    bias_grad = jnp.sum(everyone, axis=(0, 1))

    big_out = call(
        unpack_kernel,
        jax.ShapeDtypeStruct((rows, width), BF16),
        [VMEM],
        VMEM,
        (home,),
        mebibytes=8,
        flops=10**9,
        name="unpack",
    )
    return big_out, small_out, bias_grad


def solution(mesh):
    spec = P(("dp", "seq"), None)
    return jax.shard_map(
        local,
        mesh=mesh,
        in_specs=(spec,) * 5,
        out_specs=(spec, spec, P()),
        check_vma=False,
    )
```

```python
import math

import jax
import jax.numpy as jnp
from jax import lax
from jax.experimental import pallas as pl
from jax.experimental.pallas import tpu as pltpu
from jax.sharding import PartitionSpec as P

HEAD = 80
HEADS = 16
SCALE = HEAD ** (-0.5)
LANES = 128
FIRST_PART = 10
FIRST_IMAGE = 21
PAIRS = 1
IN_ROWS = 2 * HEAD
OUT_ROWS = 3 * HEAD // 2
SUM_ROWS = 8
STEPS = (((2, 2), (8, 8)), ((20, 4), (2, 2)))
SHARE = HEADS * HEAD // 4
EXPONENT = SCALE * math.log2(math.e)
F32 = jnp.float32
BF16 = jnp.bfloat16


def dot(left, right, left_dim, right_dim):
    return lax.dot_general(
        left, right, (((left_dim,), (right_dim,)), ((), ())), preferred_element_type=F32
    )


def params(mebibytes):
    return pltpu.CompilerParams(vmem_limit_bytes=mebibytes * 1024 * 1024)


def slopes_of(scores, upstream):
    exponent = jnp.exp2((scores - jnp.max(scores, axis=0, keepdims=True)) * EXPONENT)
    inverse = 1.0 / jnp.sum(exponent, axis=0, keepdims=True)
    delta = jnp.sum(exponent * upstream, axis=0, keepdims=True) * inverse
    probs = exponent * inverse
    return probs.astype(BF16), (probs * (upstream - delta)).astype(BF16)


def small_loads(qkv_hbm, grad_hbm, ids_hbm, scratch):
    sems = scratch[-1]
    sources = (qkv_hbm, grad_hbm, ids_hbm)
    return [pltpu.make_async_copy(sources[at], scratch[at], sems.at[at]) for at in range(3)]


def small_images(loads, out_hbm, kept_hbm, given_hbm, core, pairs, scratch):
    qkv, grads, ids_ref, qkv_t, grad_t, out_t, out, query_t, kept, given, sems = scratch
    rows = qkv.shape[0]
    for load in loads:
        load.wait()
    ids = jnp.broadcast_to(ids_ref[...].astype(F32), (rows, rows))
    allowed = ids == ids.T
    qkv_t[...] = qkv[...].T
    grad_t[...] = grads[...].T

    def place(head, which=0, count=3):
        first = count * HEAD * head + HEAD * which
        return pl.ds(first if isinstance(first, int) else pl.multiple_of(first, 16), HEAD)

    def some(heads):
        query, key, value = ([qkv_t[place(head, which)] for head in heads] for which in range(3))
        grad = [grad_t[place(head, 0, 1)] for head in heads]
        scores = [jnp.where(allowed, dot(*pair, 0, 0), -1e30) for pair in zip(key, query)]
        upstream = [dot(*pair, 0, 0) for pair in zip(value, grad)]
        weights, slopes = zip(*[slopes_of(*pair) for pair in zip(scores, upstream)])
        query_grad = [(dot(*pair, 1, 0) * SCALE).astype(BF16) for pair in zip(key, slopes)]
        key_grad = [(dot(*pair, 1, 1) * SCALE).astype(BF16) for pair in zip(query, slopes)]
        value_grad = [dot(*pair, 1, 1).astype(BF16) for pair in zip(grad, weights)]
        for at, head in enumerate(heads):
            query_t[place(head, 0, 1)] = query_grad[at]
            for which, result in enumerate((query_grad, key_grad, value_grad)):
                out_t[place(head, which)] = result[at]

    if pairs == HEADS // 2:
        some(range(HEADS))
    else:

        @pl.loop(0, pairs)
        def _(step):
            some([2 * step, 2 * step + 1])

        @pl.loop(2 * pairs, HEADS)
        def _(step):
            some([step])

    sums = dot(jnp.ones((8, rows), BF16), query_t[...], 1, 1)[:1]
    half = HEADS * HEAD // 2
    upper = lax.axis_index("dp") // STEPS[core][0][1] % 2
    kept[...] = jnp.where(upper == 1, sums[:, half:], sums[:, :half])
    given[...] = jnp.where(upper == 1, sums[:, :half], sums[:, half:])
    out[...] = out_t[...].T
    stores = [
        pltpu.make_async_copy(out, out_hbm, sems.at[0]),
        pltpu.make_async_copy(kept, kept_hbm, sems.at[1]),
        pltpu.make_async_copy(given, given_hbm, sems.at[2]),
    ]
    for store in stores:
        store.start()
    for store in stores:
        store.wait()


def first_kernel(
    qkv_hbm,
    grad_hbm,
    small_qkv,
    small_grad,
    ids_hbm,
    out_hbm,
    small_out,
    kept_hbm,
    given_hbm,
    qkv,
    grad,
    packed,
    in_sems,
    out_sems,
    *scratch,
):
    parts = in_sems.shape[1]
    heads = HEADS // parts
    wide, narrow = 3 * HEAD * heads, HEAD * heads
    loads = []
    for part in range(parts):
        columns = pl.ds(part * wide, wide)
        loads.append(
            pltpu.make_async_copy(qkv_hbm.at[:, columns], qkv.at[:, columns], in_sems.at[0, part])
        )
        columns = pl.ds(part * narrow, narrow)
        loads.append(
            pltpu.make_async_copy(grad_hbm.at[:, columns], grad.at[:, columns], in_sems.at[1, part])
        )
    for load in loads:
        load.start()
    late = lax.axis_index("dp") % 2 == 1
    after = small_loads(small_qkv, small_grad, ids_hbm, scratch)

    @pl.when(late)
    def _():
        for load in after:
            load.start()

    stores = []
    for part in range(parts):
        loads[2 * part].wait()
        loads[2 * part + 1].wait()
        turned = qkv[:, part * wide : (part + 1) * wide].T
        turned_grad = grad[:, part * narrow : (part + 1) * narrow].T
        for index in range(heads):
            first = 3 * HEAD * index
            left = turned[first : first + 2 * HEAD]
            right = jnp.concatenate(
                [
                    turned[first + 2 * HEAD : first + 3 * HEAD],
                    turned_grad[HEAD * index : HEAD * (index + 1)],
                ],
                axis=0,
            )
            packed[part * heads + index] = jnp.concatenate([left, right], axis=1)
        done = pl.ds(part * heads, heads)
        stores.append(pltpu.make_async_copy(packed.at[done], out_hbm.at[done], out_sems.at[part]))
        stores[-1].start()

    @pl.when(late)
    def _():
        small_images(after, small_out, kept_hbm, given_hbm, 1, PAIRS, scratch)

    for store in stores:
        store.wait()


def second_kernel(
    small_qkv, small_grad, ids_hbm, before, kept_before, given_before, small_out, kept_hbm, given_hbm, *scratch
):
    @pl.when(lax.axis_index("dp") % 2 == 0)
    def _():
        loads = small_loads(small_qkv, small_grad, ids_hbm, scratch)
        for load in loads:
            load.start()
        small_images(loads, small_out, kept_hbm, given_hbm, 0, HEADS // 2, scratch)


def pieces(row):
    high = row.astype(BF16).astype(F32)
    return jnp.concatenate([high, (row - high).astype(BF16).astype(F32)], axis=0)


def big_kernel(in_ref, sums_ref, out_ref, feat):
    pairs = in_ref.shape[0] // 2
    half = LANES // 2
    for pair in range(pairs):
        one, two = in_ref[2 * pair], in_ref[2 * pair + 1]
        columns = slice(LANES * pair, LANES * (pair + 1))
        feat[:IN_ROWS, columns] = jnp.concatenate([one[:, :half], two[:, :half]], axis=1)
        feat[IN_ROWS:, columns] = jnp.concatenate([one[:, half:], two[:, half:]], axis=1)
    query, key, value, grad = (feat[HEAD * which : HEAD * (which + 1)] for which in range(4))
    length = key.shape[1]
    weights, slopes = slopes_of(dot(key.T, query, 1, 0), dot(value.T, grad, 1, 0))
    query_grad = (dot(key, slopes, 1, 0) * SCALE).astype(BF16)
    key_grad = dot(query, slopes, 1, 1) * SCALE
    value_grad = dot(grad, weights, 1, 1)
    big_row = dot(jnp.ones((8, length), BF16), query_grad, 1, 1)[:1]
    big_row = jnp.concatenate([big_row, jnp.zeros((1, LANES - HEAD), F32)], axis=1)
    extra = pieces(jnp.concatenate([sums_ref[...], big_row], axis=0))
    whole = jnp.concatenate([query_grad.astype(F32), key_grad, value_grad], axis=0)
    for pair in range(pairs):
        block = whole[:, LANES * pair : LANES * (pair + 1)]
        upper, lower = block[:OUT_ROWS], block[OUT_ROWS:]
        one = jnp.concatenate([upper[:, :half], lower[:, :half]], axis=1)
        two = jnp.concatenate([upper[:, half:], lower[:, half:]], axis=1)
        out_ref[2 * pair] = jnp.concatenate([one, extra], axis=0).astype(BF16)
        out_ref[2 * pair + 1] = jnp.concatenate([two, extra], axis=0).astype(BF16)


def spread_kernel(in_ref, out_ref):
    image = lax.axis_index("dp")
    quarters = [image // first % 2 * 2 + image // second % 2 for (_, first), (_, second) in STEPS]
    quarter = jnp.where(image % 2 == 0, *quarters)
    sums = in_ref[:, OUT_ROWS:].astype(F32)
    sums = sums[:, : SUM_ROWS // 2] + sums[:, SUM_ROWS // 2 :]
    share = jnp.sum(sums[:, :3], axis=0)
    share = jnp.concatenate([share[at : at + 1] for at in range(3)], axis=1)[:, :SHARE]
    columns = lax.broadcasted_iota(jnp.int32, (1, HEADS * HEAD), 1) - quarter * SHARE
    share = jnp.concatenate([share] * 4, axis=1)
    big = jnp.concatenate([sums[head, 3:, :HEAD] for head in range(HEADS)], axis=1)
    total = big + jnp.where((columns >= 0) & (columns < SHARE), share, 0.0)
    out_ref[...] = jnp.broadcast_to(total[None], out_ref.shape)


def unpack_kernel(in_ref, out_ref):
    half = LANES // 2
    parts = []
    for head in range(HEADS):
        block = in_ref[head].astype(F32)[:OUT_ROWS]
        parts.append(jnp.concatenate([block[:, :half], block[:, half:]], axis=0).astype(BF16))
    out_ref[...] = jnp.concatenate(parts, axis=0).T


def call(kernel, shapes, in_specs, out_specs, operands, scratch=(), mebibytes=60, flops=0, name=None, aliases=None):
    return pl.pallas_call(
        kernel,
        out_shape=shapes,
        in_specs=in_specs,
        out_specs=out_specs,
        scratch_shapes=scratch,
        compiler_params=params(mebibytes),
        cost_estimate=pl.CostEstimate(flops=flops, bytes_accessed=2**20, transcendentals=0),
        input_output_aliases=aliases or {},
        name=name,
    )(*operands)


VMEM = pl.BlockSpec(memory_space=pltpu.VMEM)
ANY = pl.BlockSpec(memory_space=pl.ANY)


def halved(given, images, step, cores):
    pairs = [(at, at ^ STEPS[at % 2][step][0]) for at in range(images) if at % 2 in cores]
    return lax.ppermute(given, "dp", pairs)


def local(big_qkv, big_grad, small_qkv, small_grad, small_ids):
    rows = big_qkv.shape[0]
    small_rows = small_qkv.shape[0]
    images = lax.axis_size("dp")
    parts = lax.axis_size("seq")
    length = rows * parts
    ring = [[(at + FIRST_PART) % parts for at in range(parts)]]
    plane = [[(at + FIRST_IMAGE) % images for at in range(images)]]
    width = 3 * HEAD * HEADS
    image = lax.axis_index("dp")

    small_scratch = [
        pltpu.VMEM((small_rows, width), BF16),
        pltpu.VMEM((small_rows, HEAD * HEADS), BF16),
        pltpu.VMEM((1, small_rows), jnp.int32),
        pltpu.VMEM((width, small_rows), BF16),
        pltpu.VMEM((HEAD * HEADS, small_rows), BF16),
        pltpu.VMEM((width, small_rows), BF16),
        pltpu.VMEM((small_rows, width), BF16),
        pltpu.VMEM((HEAD * HEADS, small_rows), BF16),
        pltpu.VMEM((1, HEAD * HEADS // 2), F32),
        pltpu.VMEM((1, HEAD * HEADS // 2), F32),
        pltpu.SemaphoreType.DMA((3,)),
    ]
    small_shape = jax.ShapeDtypeStruct((small_rows, width), BF16)
    sum_shapes = [jax.ShapeDtypeStruct((1, HEADS * HEAD // 2), F32)] * 2
    sent, small_out, *sums = call(
        first_kernel,
        [jax.ShapeDtypeStruct((HEADS, IN_ROWS, LANES), BF16), small_shape, *sum_shapes],
        [ANY] * 5,
        [ANY] * 4,
        (big_qkv, big_grad, small_qkv, small_grad, small_ids),
        [
            pltpu.VMEM((rows, width), BF16),
            pltpu.VMEM((rows, HEAD * HEADS), BF16),
            pltpu.VMEM((HEADS, IN_ROWS, LANES), BF16),
            pltpu.SemaphoreType.DMA((2, 2)),
            pltpu.SemaphoreType.DMA((2,)),
            *small_scratch,
        ],
        name="pack",
    )
    late = lax.cond(
        image % 2 == 1, lambda given: halved(given, images, 0, (1,)), lambda given: given, sums[1]
    )
    sent, late = lax.optimization_barrier((sent, late))
    got = lax.all_to_all(sent, "seq", 0, 0, axis_index_groups=ring, tiled=True)

    small_out, *sums = call(
        second_kernel,
        [small_shape, *sum_shapes],
        [ANY] * 6,
        [ANY] * 3,
        (small_qkv, small_grad, small_ids, small_out, *sums),
        small_scratch,
        flops=10**10,
        name="small",
        aliases={3: 0, 4: 1, 5: 2},
    )

    early = halved(sums[1], images, 0, (0,))
    sums = (sums[0] + jnp.where(image % 2 == 1, late, early)).reshape(2 * SHARE)
    upper = jnp.where(image % 2 == 0, *[image // STEPS[core][1][1] % 2 for core in range(2)])
    kept = lax.dynamic_slice(sums, (upper * SHARE,), (SHARE,))
    given = lax.dynamic_slice(sums, ((1 - upper) * SHARE,), (SHARE,))
    sums = kept + halved(given, images, 1, (0, 1))
    sums = jnp.pad(sums, (0, 3 * LANES - SHARE)).reshape(3, LANES)

    back = call(
        big_kernel,
        jax.ShapeDtypeStruct((parts, OUT_ROWS + SUM_ROWS, LANES), BF16),
        [VMEM, VMEM],
        VMEM,
        (got, sums),
        mebibytes=40,
        scratch=[pltpu.VMEM((4 * HEAD, length), BF16)],
        flops=10**10,
        name="big",
    )
    home = lax.all_to_all(back, "seq", 0, 0, axis_index_groups=ring, tiled=True)

    total = call(
        spread_kernel,
        jax.ShapeDtypeStruct((images, 1, HEADS * HEAD), F32),
        [VMEM],
        VMEM,
        (home,),
        mebibytes=8,
        name="spread",
    )
    everyone = lax.all_to_all(total, "dp", 0, 0, axis_index_groups=plane, tiled=True)
    bias_grad = jnp.sum(everyone, axis=(0, 1))

    big_out = call(
        unpack_kernel,
        jax.ShapeDtypeStruct((rows, width), BF16),
        [VMEM],
        VMEM,
        (home,),
        mebibytes=8,
        flops=10**9,
        name="unpack",
    )
    return big_out, small_out, bias_grad


def solution(mesh):
    spec = P(("dp", "seq"), None)
    return jax.shard_map(
        local,
        mesh=mesh,
        in_specs=(spec,) * 5,
        out_specs=(spec, spec, P()),
        check_vma=False,
    )
```

```python
import math

import jax
import jax.numpy as jnp
from jax import lax
from jax.experimental import pallas as pl
from jax.experimental.pallas import tpu as pltpu
from jax.sharding import PartitionSpec as P

HEAD = 80
HEADS = 16
SCALE = HEAD ** (-0.5)
LANES = 128
FIRST_PART = 10
FIRST_IMAGE = 21
TOGETHER = 1
IN_ROWS = 2 * HEAD
OUT_ROWS = 3 * HEAD // 2
SUM_ROWS = 8
STEPS = (((2, 2), (8, 8)), ((20, 4), (2, 2)))
SHARE = HEADS * HEAD // 4
EXPONENT = SCALE * math.log2(math.e)
F32 = jnp.float32
BF16 = jnp.bfloat16


def dot(left, right, left_dim, right_dim):
    return lax.dot_general(
        left, right, (((left_dim,), (right_dim,)), ((), ())), preferred_element_type=F32
    )


def params(mebibytes):
    return pltpu.CompilerParams(vmem_limit_bytes=mebibytes * 1024 * 1024)


def slopes_of(scores, upstream):
    exponent = jnp.exp2((scores - jnp.max(scores, axis=0, keepdims=True)) * EXPONENT)
    inverse = 1.0 / jnp.sum(exponent, axis=0, keepdims=True)
    delta = jnp.sum(exponent * upstream, axis=0, keepdims=True) * inverse
    probs = exponent * inverse
    return probs.astype(BF16), (probs * (upstream - delta)).astype(BF16)


def small_loads(qkv_hbm, grad_hbm, ids_hbm, scratch):
    sems = scratch[-1]
    sources = (qkv_hbm, grad_hbm, ids_hbm)
    return [pltpu.make_async_copy(sources[at], scratch[at], sems.at[at]) for at in range(3)]


def small_images(loads, out_hbm, kept_hbm, given_hbm, core, together, scratch):
    qkv, grads, ids_ref, qkv_t, grad_t, out_t, out, query_t, kept, given, sems = scratch
    rows = qkv.shape[0]
    for load in loads:
        load.wait()
    ids = jnp.broadcast_to(ids_ref[...].astype(F32), (rows, rows))
    allowed = ids == ids.T
    qkv_t[...] = qkv[...].T
    grad_t[...] = grads[...].T

    def place(head, which=0, count=3):
        first = count * HEAD * head + HEAD * which
        return pl.ds(first if isinstance(first, int) else pl.multiple_of(first, 16), HEAD)

    def some(heads):
        query, key, value = ([qkv_t[place(head, which)] for head in heads] for which in range(3))
        grad = [grad_t[place(head, 0, 1)] for head in heads]
        scores = [jnp.where(allowed, dot(*pair, 0, 0), -1e30) for pair in zip(key, query)]
        upstream = [dot(*pair, 0, 0) for pair in zip(value, grad)]
        weights, slopes = zip(*[slopes_of(*pair) for pair in zip(scores, upstream)])
        query_grad = [(dot(*pair, 1, 0) * SCALE).astype(BF16) for pair in zip(key, slopes)]
        key_grad = [(dot(*pair, 1, 1) * SCALE).astype(BF16) for pair in zip(query, slopes)]
        value_grad = [dot(*pair, 1, 1).astype(BF16) for pair in zip(grad, weights)]
        for at, head in enumerate(heads):
            query_t[place(head, 0, 1)] = query_grad[at]
            for which, result in enumerate((query_grad, key_grad, value_grad)):
                out_t[place(head, which)] = result[at]

    if together == HEADS:
        some(range(HEADS))
    else:

        @pl.loop(0, HEADS // together)
        def _(step):
            some([step * together + at for at in range(together)])

    sums = dot(jnp.ones((8, rows), BF16), query_t[...], 1, 1)[:1]
    half = HEADS * HEAD // 2
    upper = lax.axis_index("dp") // STEPS[core][0][1] % 2
    kept[...] = jnp.where(upper == 1, sums[:, half:], sums[:, :half])
    given[...] = jnp.where(upper == 1, sums[:, :half], sums[:, half:])
    out[...] = out_t[...].T
    stores = [
        pltpu.make_async_copy(out, out_hbm, sems.at[0]),
        pltpu.make_async_copy(kept, kept_hbm, sems.at[1]),
        pltpu.make_async_copy(given, given_hbm, sems.at[2]),
    ]
    for store in stores:
        store.start()
    for store in stores:
        store.wait()


def first_kernel(
    qkv_hbm,
    grad_hbm,
    small_qkv,
    small_grad,
    ids_hbm,
    out_hbm,
    small_out,
    kept_hbm,
    given_hbm,
    qkv,
    grad,
    packed,
    in_sems,
    out_sems,
    *scratch,
):
    parts = in_sems.shape[1]
    heads = HEADS // parts
    wide, narrow = 3 * HEAD * heads, HEAD * heads
    loads = []
    for part in range(parts):
        columns = pl.ds(part * wide, wide)
        loads.append(
            pltpu.make_async_copy(qkv_hbm.at[:, columns], qkv.at[:, columns], in_sems.at[0, part])
        )
        columns = pl.ds(part * narrow, narrow)
        loads.append(
            pltpu.make_async_copy(grad_hbm.at[:, columns], grad.at[:, columns], in_sems.at[1, part])
        )
    for load in loads:
        load.start()
    late = lax.axis_index("dp") % 2 == 1
    after = small_loads(small_qkv, small_grad, ids_hbm, scratch)

    @pl.when(late)
    def _():
        for load in after:
            load.start()

    stores = []
    for part in range(parts):
        loads[2 * part].wait()
        loads[2 * part + 1].wait()
        turned = qkv[:, part * wide : (part + 1) * wide].T
        turned_grad = grad[:, part * narrow : (part + 1) * narrow].T
        for index in range(heads):
            first = 3 * HEAD * index
            left = turned[first : first + 2 * HEAD]
            right = jnp.concatenate(
                [
                    turned[first + 2 * HEAD : first + 3 * HEAD],
                    turned_grad[HEAD * index : HEAD * (index + 1)],
                ],
                axis=0,
            )
            packed[part * heads + index] = jnp.concatenate([left, right], axis=1)
        done = pl.ds(part * heads, heads)
        stores.append(pltpu.make_async_copy(packed.at[done], out_hbm.at[done], out_sems.at[part]))
        stores[-1].start()

    @pl.when(late)
    def _():
        small_images(after, small_out, kept_hbm, given_hbm, 1, TOGETHER, scratch)

    for store in stores:
        store.wait()


def second_kernel(
    small_qkv, small_grad, ids_hbm, before, kept_before, given_before, small_out, kept_hbm, given_hbm, *scratch
):
    @pl.when(lax.axis_index("dp") % 2 == 0)
    def _():
        loads = small_loads(small_qkv, small_grad, ids_hbm, scratch)
        for load in loads:
            load.start()
        small_images(loads, small_out, kept_hbm, given_hbm, 0, HEADS, scratch)


def pieces(row):
    high = row.astype(BF16).astype(F32)
    return jnp.concatenate([high, (row - high).astype(BF16).astype(F32)], axis=0)


def big_kernel(in_ref, sums_ref, out_ref, feat):
    pairs = in_ref.shape[0] // 2
    half = LANES // 2
    for pair in range(pairs):
        one, two = in_ref[2 * pair], in_ref[2 * pair + 1]
        columns = slice(LANES * pair, LANES * (pair + 1))
        feat[:IN_ROWS, columns] = jnp.concatenate([one[:, :half], two[:, :half]], axis=1)
        feat[IN_ROWS:, columns] = jnp.concatenate([one[:, half:], two[:, half:]], axis=1)
    query, key, value, grad = (feat[HEAD * which : HEAD * (which + 1)] for which in range(4))
    length = key.shape[1]
    weights, slopes = slopes_of(dot(key.T, query, 1, 0), dot(value.T, grad, 1, 0))
    query_grad = (dot(key, slopes, 1, 0) * SCALE).astype(BF16)
    key_grad = dot(query, slopes, 1, 1) * SCALE
    value_grad = dot(grad, weights, 1, 1)
    big_row = dot(jnp.ones((8, length), BF16), query_grad, 1, 1)[:1]
    big_row = jnp.concatenate([big_row, jnp.zeros((1, LANES - HEAD), F32)], axis=1)
    extra = pieces(jnp.concatenate([sums_ref[...], big_row], axis=0))
    whole = jnp.concatenate([query_grad.astype(F32), key_grad, value_grad], axis=0)
    for pair in range(pairs):
        block = whole[:, LANES * pair : LANES * (pair + 1)]
        upper, lower = block[:OUT_ROWS], block[OUT_ROWS:]
        one = jnp.concatenate([upper[:, :half], lower[:, :half]], axis=1)
        two = jnp.concatenate([upper[:, half:], lower[:, half:]], axis=1)
        out_ref[2 * pair] = jnp.concatenate([one, extra], axis=0).astype(BF16)
        out_ref[2 * pair + 1] = jnp.concatenate([two, extra], axis=0).astype(BF16)


def spread_kernel(in_ref, out_ref):
    image = lax.axis_index("dp")
    quarters = [image // first % 2 * 2 + image // second % 2 for (_, first), (_, second) in STEPS]
    quarter = jnp.where(image % 2 == 0, *quarters)
    sums = in_ref[:, OUT_ROWS:].astype(F32)
    sums = sums[:, : SUM_ROWS // 2] + sums[:, SUM_ROWS // 2 :]
    share = jnp.sum(sums[:, :3], axis=0)
    share = jnp.concatenate([share[at : at + 1] for at in range(3)], axis=1)[:, :SHARE]
    columns = lax.broadcasted_iota(jnp.int32, (1, HEADS * HEAD), 1) - quarter * SHARE
    share = jnp.concatenate([share] * 4, axis=1)
    big = jnp.concatenate([sums[head, 3:, :HEAD] for head in range(HEADS)], axis=1)
    total = big + jnp.where((columns >= 0) & (columns < SHARE), share, 0.0)
    out_ref[...] = jnp.broadcast_to(total[None], out_ref.shape)


def unpack_kernel(in_ref, out_ref):
    half = LANES // 2
    parts = []
    for head in range(HEADS):
        block = in_ref[head].astype(F32)[:OUT_ROWS]
        parts.append(jnp.concatenate([block[:, :half], block[:, half:]], axis=0).astype(BF16))
    out_ref[...] = jnp.concatenate(parts, axis=0).T


def call(kernel, shapes, in_specs, out_specs, operands, scratch=(), mebibytes=60, flops=0, name=None, aliases=None):
    return pl.pallas_call(
        kernel,
        out_shape=shapes,
        in_specs=in_specs,
        out_specs=out_specs,
        scratch_shapes=scratch,
        compiler_params=params(mebibytes),
        cost_estimate=pl.CostEstimate(flops=flops, bytes_accessed=2**20, transcendentals=0),
        input_output_aliases=aliases or {},
        name=name,
    )(*operands)


VMEM = pl.BlockSpec(memory_space=pltpu.VMEM)
ANY = pl.BlockSpec(memory_space=pl.ANY)


def halved(given, images, step, cores):
    pairs = [(at, at ^ STEPS[at % 2][step][0]) for at in range(images) if at % 2 in cores]
    return lax.ppermute(given, "dp", pairs)


def local(big_qkv, big_grad, small_qkv, small_grad, small_ids):
    rows = big_qkv.shape[0]
    small_rows = small_qkv.shape[0]
    images = lax.axis_size("dp")
    parts = lax.axis_size("seq")
    length = rows * parts
    ring = [[(at + FIRST_PART) % parts for at in range(parts)]]
    plane = [[(at + FIRST_IMAGE) % images for at in range(images)]]
    width = 3 * HEAD * HEADS
    image = lax.axis_index("dp")

    small_scratch = [
        pltpu.VMEM((small_rows, width), BF16),
        pltpu.VMEM((small_rows, HEAD * HEADS), BF16),
        pltpu.VMEM((1, small_rows), jnp.int32),
        pltpu.VMEM((width, small_rows), BF16),
        pltpu.VMEM((HEAD * HEADS, small_rows), BF16),
        pltpu.VMEM((width, small_rows), BF16),
        pltpu.VMEM((small_rows, width), BF16),
        pltpu.VMEM((HEAD * HEADS, small_rows), BF16),
        pltpu.VMEM((1, HEAD * HEADS // 2), F32),
        pltpu.VMEM((1, HEAD * HEADS // 2), F32),
        pltpu.SemaphoreType.DMA((3,)),
    ]
    small_shape = jax.ShapeDtypeStruct((small_rows, width), BF16)
    sum_shapes = [jax.ShapeDtypeStruct((1, HEADS * HEAD // 2), F32)] * 2
    sent, small_out, *sums = call(
        first_kernel,
        [jax.ShapeDtypeStruct((HEADS, IN_ROWS, LANES), BF16), small_shape, *sum_shapes],
        [ANY] * 5,
        [ANY] * 4,
        (big_qkv, big_grad, small_qkv, small_grad, small_ids),
        [
            pltpu.VMEM((rows, width), BF16),
            pltpu.VMEM((rows, HEAD * HEADS), BF16),
            pltpu.VMEM((HEADS, IN_ROWS, LANES), BF16),
            pltpu.SemaphoreType.DMA((2, 2)),
            pltpu.SemaphoreType.DMA((2,)),
            *small_scratch,
        ],
        name="pack",
    )
    late = lax.cond(
        image % 2 == 1, lambda given: halved(given, images, 0, (1,)), lambda given: given, sums[1]
    )
    sent, late = lax.optimization_barrier((sent, late))
    got = lax.all_to_all(sent, "seq", 0, 0, axis_index_groups=ring, tiled=True)

    small_out, *sums = call(
        second_kernel,
        [small_shape, *sum_shapes],
        [ANY] * 6,
        [ANY] * 3,
        (small_qkv, small_grad, small_ids, small_out, *sums),
        small_scratch,
        mebibytes=40,
        flops=10**10,
        name="small",
        aliases={3: 0, 4: 1, 5: 2},
    )

    early = halved(sums[1], images, 0, (0,))
    sums = (sums[0] + jnp.where(image % 2 == 1, late, early)).reshape(2 * SHARE)
    upper = jnp.where(image % 2 == 0, *[image // STEPS[core][1][1] % 2 for core in range(2)])
    kept = lax.dynamic_slice(sums, (upper * SHARE,), (SHARE,))
    given = lax.dynamic_slice(sums, ((1 - upper) * SHARE,), (SHARE,))
    sums = kept + halved(given, images, 1, (0, 1))
    sums = jnp.pad(sums, (0, 3 * LANES - SHARE)).reshape(3, LANES)

    back = call(
        big_kernel,
        jax.ShapeDtypeStruct((parts, OUT_ROWS + SUM_ROWS, LANES), BF16),
        [VMEM, VMEM],
        VMEM,
        (got, sums),
        mebibytes=40,
        scratch=[pltpu.VMEM((4 * HEAD, length), BF16)],
        flops=10**10,
        name="big",
    )
    home = lax.all_to_all(back, "seq", 0, 0, axis_index_groups=ring, tiled=True)

    total = call(
        spread_kernel,
        jax.ShapeDtypeStruct((images, 1, HEADS * HEAD), F32),
        [VMEM],
        VMEM,
        (home,),
        mebibytes=8,
        name="spread",
    )
    everyone = lax.all_to_all(total, "dp", 0, 0, axis_index_groups=plane, tiled=True)
    bias_grad = jnp.sum(everyone, axis=(0, 1))

    big_out = call(
        unpack_kernel,
        jax.ShapeDtypeStruct((rows, width), BF16),
        [VMEM],
        VMEM,
        (home,),
        mebibytes=8,
        flops=10**9,
        name="unpack",
    )
    return big_out, small_out, bias_grad


def solution(mesh):
    spec = P(("dp", "seq"), None)
    return jax.shard_map(
        local,
        mesh=mesh,
        in_specs=(spec,) * 5,
        out_specs=(spec, spec, P()),
        check_vma=False,
    )
```
